256 devices in a mesh: ty: 16 (over z_lo, x, core), tx: 16 (over z_hi, y).
Axes of the slice: x: 4, y: 4, z: 8 (z_hi: 4, z_lo: 2; z = z_hi * 2 + z_lo), core: 2. Of those that a mesh axis runs over, the one named last changes fastest.
Arguments:
- sky_tile: bfloat16 [6, 2048, 4096], P(None, 'ty', 'tx'), may hold values from -6 to 6
- request_offset: int32 [16, 16, 8, 2, 2], P('ty', 'tx'), may hold values from 0 to 192, as said below
- request_count: int32 [16, 16, 8], P('ty', 'tx'), may hold values from 0 to 2, as said below
- tile_target: float32 [16, 16, 8, 512], P('ty', 'tx'), may hold values from -6 to 6
- cut_target: float32 [16, 16, 8, 1024], P('ty', 'tx'), may hold values from -6 to 6
- w_first: bfloat16 [24, 64], replicated, may hold values from -1.25 to 1.25
- w_second: bfloat16 [256, 128], replicated, may hold values from -0.375 to 0.375
- w_third: bfloat16 [512, 256], replicated, may hold values from -0.25 to 0.25
- w_head: bfloat16 [8, 256], replicated, may hold values from -0.375 to 0.375
Outputs:
- grad_first: float32 [24, 64], replicated
- grad_second: float32 [256, 128], replicated
- grad_third: float32 [512, 256], replicated
- grad_head: float32 [8, 256], replicated
- cut_pred: bfloat16 [16, 16, 8, 1024], P('ty', 'tx')
The draws below stay inside these ranges and needn't reach their ends.
Inputs may be any that keep to these rules, and one draw needn't show every extreme that they name: request_count[r, c, k] of the 2 slots of direction k are used; it is zero where that neighbour lies outside the grid, and some tile uses all 2 slots of all eight directions. `request_offset`: offsets are in the frame of the neighbouring tile; every cutout lies within 96 pixels of the border that this neighbour shares with tile (r, c) along each axis where the direction moves.
All inputs are finite; a program needn't handle non-finite values.
Results may differ from the reference program's by a relative error of at most 0.002.
The reference program's roundings to bfloat16 on the way count: a program that leaves them out, or rounds other values in their place, can miss the bound.
Values may be sent and summed in bfloat16 or wider, within the bound.
A program may use at most 128 MiB of HBM per device.

```python
import jax
import jax.numpy as jnp
from jax import lax

BANDS = 6
C1 = 64
C2 = 128
C3 = 256
NOUT = 8
CUT = 64
RIM = 96
TH = 128
CAP = 2
TW = 256
GY = 16
GX = 16
TILES = 256
QT = 512
QC = 64
SLOTS = 16


def draw_request_count(key, part):
    first_draw = jax.random.randint(jax.random.fold_in(key, 1), (GY, GX, 8), 0, CAP + 1)
    extra_draw = jax.random.randint(jax.random.fold_in(key, 2), (GY, GX, 1), 0, CAP + 1)
    counts = jnp.minimum(first_draw + extra_draw, CAP)
    step_rows = jnp.array([-1, -1, -1, 0, 0, 1, 1, 1], jnp.int32)
    step_cols = jnp.array([-1, 0, 1, -1, 1, -1, 0, 1], jnp.int32)
    row_index = jnp.arange(GY, dtype=jnp.int32)[:, None, None] + step_rows
    col_index = jnp.arange(GX, dtype=jnp.int32)[None, :, None] + step_cols
    inside = (row_index >= 0) & (row_index < GY) & (col_index >= 0) & (col_index < GX)
    full_row = jax.random.randint(jax.random.fold_in(key, 3), (), 1, GY - 1)
    full_col = jax.random.randint(jax.random.fold_in(key, 4), (), 1, GX - 1)
    chosen = (jnp.arange(GY, dtype=jnp.int32)[:, None, None] == full_row) & (jnp.arange(GX, dtype=jnp.int32)[None, :, None] == full_col)
    counts = jnp.where(chosen, CAP, counts)
    return jnp.where(inside, counts, 0).astype(jnp.int32)


def draw_request_offset(key, part):
    step_rows = jnp.array([-1, -1, -1, 0, 0, 1, 1, 1], jnp.int32)[:, None]
    step_cols = jnp.array([-1, 0, 1, -1, 1, -1, 0, 1], jnp.int32)[:, None]
    low_rows = jnp.where(step_rows < 0, TH - RIM, 0)
    high_rows = jnp.where(step_rows > 0, RIM - CUT, TH - CUT)
    low_cols = jnp.where(step_cols < 0, TW - RIM, 0)
    high_cols = jnp.where(step_cols > 0, RIM - CUT, TW - CUT)
    row_draw = jax.random.randint(jax.random.fold_in(key, 5), (GY, GX, 8, CAP), low_rows, high_rows + 1)
    col_draw = jax.random.randint(jax.random.fold_in(key, 6), (GY, GX, 8, CAP), low_cols, high_cols + 1)
    return jnp.stack([row_draw, col_draw], axis=3).astype(jnp.int32)


def level_of(rng, shape, cuts, smallest, largest):
    level = 1.0
    for dim, shards_of in cuts:
        steps = jax.random.uniform(jax.random.fold_in(jax.random.fold_in(rng, 6), dim), (shards_of,), jnp.float32, smallest / len(cuts), largest / len(cuts))
        level = level * jnp.repeat(jnp.exp(steps), shape[dim] // shards_of).reshape((-1,) + (1,) * (len(shape) - 1 - dim))
    return level


def gaussian(rng, extent, scale, reach, pieces=(), kind=jnp.bfloat16):
    values = scale * jax.random.normal(rng, extent, jnp.float32)
    if pieces:
        values = values * level_of(rng, extent, pieces, -0.22, 0.18)
    return jnp.clip(values, -reach, reach).astype(kind)


def setup_inputs(seed: int = 0) -> dict:
    streams_of = jax.random.split(jax.random.key(seed), 10)
    return {
        "sky_tile": gaussian(streams_of[0], (BANDS, GY * TH, GX * TW), 1.0, 6.0, ((1, 16), (2, 16))),
        "request_offset": draw_request_offset(jax.random.fold_in(streams_of[9], 71), 0),
        "request_count": draw_request_count(jax.random.fold_in(streams_of[9], 71), 0),
        "tile_target": gaussian(streams_of[3], (GY, GX, NOUT, QT), 1.0, 6.0, ((0, 16), (1, 16)), jnp.float32),
        "cut_target": gaussian(streams_of[4], (GY, GX, NOUT, SLOTS * QC), 1.0, 6.0, ((0, 16), (1, 16)), jnp.float32),
        "w_first": gaussian(streams_of[5], (4 * BANDS, C1), (4 * BANDS) ** -0.5, 1.25),
        "w_second": gaussian(streams_of[6], (4 * C1, C2), (4 * C1) ** -0.5, 0.375),
        "w_third": gaussian(streams_of[7], (4 * C2, C3), (4 * C2) ** -0.5, 0.25),
        "w_head": gaussian(streams_of[8], (NOUT, C3), C3 ** -0.5, 0.375),
    }


DIRECTIONS = ((-1, -1), (-1, 0), (-1, 1), (0, -1), (0, 1), (1, -1), (1, 0), (1, 1))


def inner(left_mat, right_mat):
    return lax.dot_general(left_mat, right_mat, (((0,), (0,)), ((), ())), preferred_element_type=jnp.float32)


def outer(left_mat, right_mat):
    return lax.dot_general(left_mat, right_mat, (((1,), (1,)), ((), ())), preferred_element_type=jnp.float32)


def patchify(field_now):
    channels, batch_size, rows_in, cols_in = field_now.shape
    blocks = field_now.reshape(channels, batch_size, rows_in // 2, 2, cols_in // 2, 2)
    blocks = blocks.transpose(0, 3, 5, 1, 2, 4)
    return blocks.reshape(channels * 4, batch_size * (rows_in // 2) * (cols_in // 2))


def unpatchify(grads_in, shape_in):
    channels, batch_size, rows_in, cols_in = shape_in
    blocks = grads_in.reshape(channels, 2, 2, batch_size, rows_in // 2, cols_in // 2)
    blocks = blocks.transpose(0, 3, 4, 1, 5, 2)
    return blocks.reshape(channels, batch_size * rows_in * cols_in)


def activation_slope(pre_act):
    sigmoid_value = jax.nn.sigmoid(pre_act)
    return sigmoid_value * (1.0 + pre_act * (1.0 - sigmoid_value))


def forward(image_stack, weights):
    stored = []
    field_now = image_stack
    active = image_stack
    for weight_matrix in weights[:3]:
        shape_in = field_now.shape
        patches = patchify(field_now)
        pre_act = inner(weight_matrix, patches)
        active = jax.nn.silu(pre_act).astype(jnp.bfloat16)
        stored.append((patches, pre_act, shape_in))
        field_now = active.reshape(weight_matrix.shape[1], shape_in[1], shape_in[2] // 2, shape_in[3] // 2)
    predicted = jnp.dot(weights[3], active, preferred_element_type=jnp.float32)
    return stored, active, predicted


def add_terms(term_list):
    running_total = term_list[0]
    for extra_term in term_list[1:]:
        running_total = running_total + extra_term
    return running_total


def backward(path_list, weights, finish):
    results = [None, None, None, None]
    results[3] = finish(add_terms([outer(loss_grad, top_act) for stored, top_act, loss_grad in path_list]))
    deltas = []
    for stored, top_act, loss_grad in path_list:
        upward = inner(weights[3], loss_grad)
        deltas.append((upward * activation_slope(stored[2][1])).astype(jnp.bfloat16))
    for layer_index in (2, 1, 0):
        term_list = [outer(path_item[0][layer_index][0], delta_now) for path_item, delta_now in zip(path_list, deltas)]
        results[layer_index] = finish(add_terms(term_list))
        if layer_index > 0:
            fresh_deltas = []
            for path_item, delta_now in zip(path_list, deltas):
                upward = jnp.dot(weights[layer_index], delta_now, preferred_element_type=jnp.float32)
                upward = unpatchify(upward, path_item[0][layer_index][2])
                fresh_deltas.append((upward * activation_slope(path_item[0][layer_index - 1][1])).astype(jnp.bfloat16))
            deltas = fresh_deltas
    return tuple(results)


def unchanged(summed_term):
    return summed_term


def reference(sky_tile, request_offset, request_count, tile_target, cut_target, w_first, w_second, w_third, w_head):
    weights = (w_first, w_second, w_third, w_head)
    band_count = sky_tile.shape[0]
    step_rows = jnp.array([pair[0] for pair in DIRECTIONS], jnp.int32)
    step_cols = jnp.array([pair[1] for pair in DIRECTIONS], jnp.int32)
    zero_index = jnp.zeros((), jnp.int32)

    def window(row_at, col_at):
        return lax.dynamic_slice(sky_tile, (zero_index, row_at, col_at), (band_count, CUT, CUT))

    def per_tile(totals, tile_index):
        tile_row = (tile_index // GX).astype(jnp.int32)
        tile_col = (tile_index % GX).astype(jnp.int32)
        own_image = lax.dynamic_slice(sky_tile, (zero_index, tile_row * TH, tile_col * TW), (band_count, TH, TW))
        offsets = request_offset[tile_row, tile_col]
        rows_at = jnp.clip((tile_row + step_rows)[:, None] * TH + offsets[:, 0], 0, GY * TH - CUT).reshape(-1).astype(jnp.int32)
        cols_at = jnp.clip((tile_col + step_cols)[:, None] * TW + offsets[:, 1], 0, GX * TW - CUT).reshape(-1).astype(jnp.int32)
        cutouts = jax.vmap(window)(rows_at, cols_at)
        cut_stack = cutouts.transpose(1, 0, 2, 3)
        counts = request_count[tile_row, tile_col]
        valid_slots = (jnp.arange(CAP, dtype=jnp.int32)[None, :] < counts[:, None]).astype(jnp.float32).reshape(-1)
        mask_full = jnp.repeat(valid_slots, QC)
        own_stored, own_top, own_pred = forward(own_image[:, None], weights)
        own_grad = ((own_pred - tile_target[tile_row, tile_col]) / TILES).astype(jnp.bfloat16)
        cut_stored, cut_top, cut_full = forward(cut_stack, weights)
        cut_grad = ((cut_full - cut_target[tile_row, tile_col]) * mask_full / TILES).astype(jnp.bfloat16)
        grads_here = backward([(own_stored, own_top, own_grad), (cut_stored, cut_top, cut_grad)], weights, unchanged)
        new_totals = tuple(running + latest for running, latest in zip(totals, grads_here))
        return new_totals, (cut_full * mask_full).astype(jnp.bfloat16)

    initial = tuple(jnp.zeros(weight_matrix.shape, jnp.float32) for weight_matrix in weights)
    totals, predictions = lax.scan(per_tile, initial, jnp.arange(TILES, dtype=jnp.int32))
    cut_pred = predictions.reshape(GY, GX, NOUT, SLOTS * QC)
    return (totals[0], totals[1], totals[2], totals[3], cut_pred)
```

```python
import functools

import jax
import jax.numpy as jnp
from jax import lax
from jax.experimental import pallas as pl
from jax.experimental.pallas import tpu as pltpu
from jax.sharding import PartitionSpec as P

DIRECTIONS = ((-1, -1), (-1, 0), (-1, 1), (0, -1), (0, 1), (1, -1), (1, 0), (1, 1))
MESH = pl.DeviceIdType.MESH
BF = jnp.bfloat16
F32 = jnp.float32
I32 = jnp.int32
VMEM_BYTES = 56 * 1024 * 1024
ROWS = 1536


def iota(shape, dim):
    return lax.broadcasted_iota(I32, shape, dim)


def one_hot(condition, kind=BF):
    return jnp.where(condition, 1.0, 0.0).astype(kind)


def nn(a, b):
    return lax.dot_general(a, b, (((1,), (0,)), ((), ())), preferred_element_type=F32)


def nt(a, b):
    return lax.dot_general(a, b, (((1,), (1,)), ((), ())), preferred_element_type=F32)


def tn(a, b):
    return lax.dot_general(a, b, (((0,), (0,)), ((), ())), preferred_element_type=F32)


def cut_kernel(off_ref, img_ref, got_ref, msg, req, rows_sel, rows_got, cut,
               req_send, req_recv, rep_send, rep_recv):
    ty = lax.axis_index("ty")
    tx = lax.axis_index("tx")
    n_ty = lax.axis_size("ty")
    n_tx = lax.axis_size("tx")

    def device(dy, dx):
        return (lax.rem(ty + dy + n_ty, n_ty), lax.rem(tx + dx + n_tx, n_tx))

    barrier = pltpu.get_barrier_semaphore()
    for dy, dx in DIRECTIONS:
        pl.semaphore_signal(barrier, inc=1, device_id=device(dy, dx), device_id_type=MESH)

    lane = iota((8, 128), 1)
    sub = iota((8, 128), 0)
    first = lane < 64
    col_step = 8 * (lane % 8) + (lane // 8) % 8
    for k in range(8):
        r0 = jnp.where(first, off_ref[k * 4], off_ref[k * 4 + 1])
        c0 = jnp.where(first, off_ref[k * 4 + 2], off_ref[k * 4 + 3] + 256)
        msg[k] = jnp.where(sub == 0, c0 + col_step, r0 + lane % 64)

    pl.semaphore_wait(barrier, 8)

    requests = []
    for k, (dy, dx) in enumerate(DIRECTIONS):
        copy = pltpu.make_async_remote_copy(
            src_ref=msg.at[k], dst_ref=req.at[k],
            send_sem=req_send.at[k], recv_sem=req_recv.at[k],
            device_id=device(dy, dx), device_id_type=MESH,
        )
        copy.start()
        requests.append(copy)
    for copy in requests:
        copy.wait()

    for k in range(8):
        rows_sel[:, k * 128:(k + 1) * 128] = one_hot(iota((128, 128), 0) == req[k][1:2, :])
    for band in range(6):
        rows_got[band] = tn(rows_sel[...], img_ref[band])

    replies = []
    for k in (0, 2, 5, 7, 3, 4, 1, 6):
        dy, dx = DIRECTIONS[k]
        halves = []
        for p in range(2):
            pieces = []
            for block in range(8):
                at = k * 128 + p * 64 + block * 8
                for band in range(6):
                    pieces.append(rows_got[band, at:at + 8, :])
            halves.append(jnp.concatenate(pieces, axis=0).astype(BF))
        cols_sel = one_hot(iota((512, 128), 0) == req[k][0:1, :])
        cut[k] = (nn(halves[0], cols_sel[:256]) + nn(halves[1], cols_sel[256:])).astype(BF)
        copy = pltpu.make_async_remote_copy(
            src_ref=cut.at[k], dst_ref=got_ref.at[k],
            send_sem=rep_send.at[k], recv_sem=rep_recv.at[k],
            device_id=device(-dy, -dx), device_id_type=MESH,
        )
        copy.start()
        replies.append(copy)
    for copy in replies:
        copy.wait()


def exchange_cutouts(offsets, image):
    return pl.pallas_call(
        cut_kernel,
        out_shape=jax.ShapeDtypeStruct((8, 384, 128), BF),
        in_specs=[pl.BlockSpec(memory_space=pltpu.SMEM), pl.BlockSpec(memory_space=pltpu.VMEM)],
        out_specs=pl.BlockSpec(memory_space=pltpu.VMEM),
        scratch_shapes=[
            pltpu.VMEM((8, 8, 128), I32),
            pltpu.VMEM((8, 8, 128), I32),
            pltpu.VMEM((128, 1024), BF),
            pltpu.VMEM((6, 1024, 256), F32),
            pltpu.VMEM((8, 384, 128), BF),
            pltpu.SemaphoreType.DMA((8,)),
            pltpu.SemaphoreType.DMA((8,)),
            pltpu.SemaphoreType.DMA((8,)),
            pltpu.SemaphoreType.DMA((8,)),
        ],
        compiler_params=pltpu.CompilerParams(
            collective_id=0, has_side_effects=True, vmem_limit_bytes=VMEM_BYTES
        ),
        name="cutouts",
    )(offsets, image)


def first_mask():
    row = iota((512, 192), 0)
    col = iota((512, 192), 1)
    return (row // 128 == (col % 8) // 2) & ((row // 64) % 2 == col // 96)


def first_spread():
    row = iota((24, 192), 0)
    col = iota((24, 192), 1)
    return row == ((col % 48) // 8) * 4 + (col % 2) * 2 + (col // 48) % 2


def net_kernel(cnt_ref, img_ref, got_ref, own_target_ref, cut_target_ref, w1_ref, w2_ref, w3_ref, wh_ref,
               grads_ref, cut_pred_ref,
               field, place, wide1, w2, w2t, w3, w3t, act1, slope1, act2, slope2, delta1, delta2,
               target, mask, pred_all, g1, g2, g3, gh):
    up = one_hot(iota((512, 64), 0) % 64 == iota((512, 64), 1))
    wide = nn(nt(up, w1_ref[...]).astype(BF), one_hot(first_spread()))
    wide1[...] = jnp.where(first_mask(), wide, 0.0).astype(BF)
    new = iota((256, 256), 0)
    w2[...] = nn(one_hot(iota((256, 256), 1) == (new % 64) * 4 + new // 64), w2_ref[...]).astype(BF)
    new = iota((256, 256), 1)
    w2t[...] = tn(w2_ref[...], one_hot(iota((256, 256), 0) == (new % 64) * 4 + new // 64)).astype(BF)
    new = iota((512, 512), 0)
    w3[...] = nn(one_hot(iota((512, 512), 1) == (new % 128) * 4 + new // 128), w3_ref[...]).astype(BF)
    new = iota((512, 512), 1)
    w3t[...] = tn(w3_ref[...], one_hot(iota((512, 512), 0) == (new % 128) * 4 + new // 128)).astype(BF)
    wh = wh_ref[...]

    src = iota((1024, 1024), 0)
    place[...] = one_hot(iota((1024, 1024), 1) == (src % 8) * 128 + (src // 256) * 32 + (src % 256) // 8)
    lines = []
    images = [img_ref[band].astype(F32) for band in range(6)]
    for q in range(4):
        for band in range(6):
            lines.append(jnp.concatenate(
                [images[band][(4 * q + r) * 8:(4 * q + r) * 8 + 8] for r in range(4)], axis=1))
    spread = nn(jnp.concatenate(lines, axis=0).astype(BF), place[...]).astype(BF)
    for q in range(4):
        for j in range(8):
            field[j // 4, 0, (j % 4) * 48:(j % 4) * 48 + 48, q * 128:(q + 1) * 128] = (
                spread[q * 48:(q + 1) * 48, j * 128:(j + 1) * 128])
    src = iota((1024, 1024), 0)
    place[...] = one_hot(
        iota((1024, 1024), 1)
        == ((src // 8) % 8) * 128 + ((src // 64) % 2) * 64 + (src // 128) * 8 + src % 8)
    for half in range(2):
        stack = jnp.concatenate(
            [jnp.concatenate([got_ref[half * 4 + k, r * 48:(r + 1) * 48, :] for r in range(8)], axis=1)
             for k in range(4)], axis=0)
        spread = nn(stack, place[...]).astype(BF)
        for k in range(4):
            for j in range(8):
                field[j // 4, 1 + half, (j % 4) * 48:(j % 4) * 48 + 48, k * 128:(k + 1) * 128] = (
                    spread[k * 48:(k + 1) * 48, j * 128:(j + 1) * 128])

    target[0] = own_target_ref[...]
    target[1] = cut_target_ref[:, :512]
    target[2] = cut_target_ref[:, 512:]
    mask[0] = jnp.full((8, 512), 1.0, F32)
    slot = (iota((8, 128), 1) // 64)
    for k in range(8):
        mask[1 + k // 4, :, (k % 4) * 128:(k % 4) * 128 + 128] = jnp.where(slot < cnt_ref[k], 1.0, 0.0)

    g1[...] = jnp.zeros_like(g1)
    g2[...] = jnp.zeros_like(g2)
    g3[...] = jnp.zeros_like(g3)
    gh[...] = jnp.zeros_like(gh)

    def silu(pre):
        sig = 0.5 * jnp.tanh(0.5 * pre) + 0.5
        act = pre * sig
        return act.astype(BF), sig + act * (1.0 - sig)

    def part(step, carry):
        for ac in range(2):
            act1[ac], slope1[ac] = silu(nn(wide1[...], field[ac, step]))
            for ar in range(2):
                at = (ar * 2 + ac) * 128
                act2[at:at + 128], slope2[at:at + 128] = silu(nn(w2t[...], act1[ac, ar * 256:ar * 256 + 256]))
        act3, slope3 = silu(nn(w3t[...], act2[...]))
        pred = nn(wh, act3)
        used = mask[step]
        grad = ((pred - target[step]) * used * (1.0 / 256.0)).astype(BF)
        pred_all[step] = (pred * used)
        gh[...] += nt(grad, act3)
        delta3 = (tn(wh, grad) * slope3).astype(BF)
        g3[...] += nt(act2[...], delta3)
        delta2[...] = (nn(w3[...], delta3) * slope2[...]).astype(BF)
        for ac in range(2):
            for ar in range(2):
                at = (ar * 2 + ac) * 128
                rows = slice(ar * 256, ar * 256 + 256)
                g2[...] += nt(act1[ac, rows], delta2[at:at + 128])
                delta1[ac, rows] = (nn(w2[...], delta2[at:at + 128]) * slope1[ac, rows]).astype(BF)
            g1[...] += nt(delta1[ac], field[ac, step])
        return carry

    lax.fori_loop(0, 3, part, 0)

    cut_pred_ref[:, :512] = pred_all[1].astype(BF)
    cut_pred_ref[:, 512:] = pred_all[2].astype(BF)

    for phase in range(4):
        for half in range(2):
            grads_ref[pl.ds(half * 512 + phase, 128, stride=4), :] = (
                g3[phase * 128:phase * 128 + 128, half * 128:half * 128 + 128])
        grads_ref[pl.ds(1024 + phase, 64, stride=4), :] = g2[phase * 64:phase * 64 + 64, :]
    picked = jnp.where(first_mask(), g1[...], 0.0)
    folded = lax.dot_general(
        one_hot(first_spread(), F32), picked, (((1,), (1,)), ((), ())),
        precision=lax.Precision.HIGHEST, preferred_element_type=F32)
    total = lax.dot_general(
        folded, one_hot(iota((512, 128), 0) % 64 == iota((512, 128), 1), F32), (((1,), (0,)), ((), ())),
        precision=lax.Precision.HIGHEST, preferred_element_type=F32)
    grads_ref[1280:1304, :] = total
    grads_ref[1304:1312, :] = gh[:, :128]
    grads_ref[1312:1320, :] = gh[:, 128:]
    grads_ref[1320:, :] = jnp.zeros((ROWS - 1320, 128), F32)


def network(counts, image, got, own_target, cut_target, weights):
    vmem = pl.BlockSpec(memory_space=pltpu.VMEM)
    return pl.pallas_call(
        net_kernel,
        out_shape=(jax.ShapeDtypeStruct((ROWS, 128), F32), jax.ShapeDtypeStruct((8, 1024), BF)),
        in_specs=[pl.BlockSpec(memory_space=pltpu.SMEM)] + [vmem] * 8,
        out_specs=(vmem, vmem),
        scratch_shapes=[
            pltpu.VMEM((2, 3, 192, 512), BF),
            pltpu.VMEM((1024, 1024), BF),
            pltpu.VMEM((512, 192), BF),
            pltpu.VMEM((256, 128), BF),
            pltpu.VMEM((128, 256), BF),
            pltpu.VMEM((512, 256), BF),
            pltpu.VMEM((256, 512), BF),
            pltpu.VMEM((2, 512, 512), BF),
            pltpu.VMEM((2, 512, 512), F32),
            pltpu.VMEM((512, 512), BF),
            pltpu.VMEM((512, 512), F32),
            pltpu.VMEM((2, 512, 512), BF),
            pltpu.VMEM((512, 512), BF),
            pltpu.VMEM((3, 8, 512), F32),
            pltpu.VMEM((3, 8, 512), F32),
            pltpu.VMEM((3, 8, 512), F32),
            pltpu.VMEM((512, 192), F32),
            pltpu.VMEM((256, 128), F32),
            pltpu.VMEM((512, 256), F32),
            pltpu.VMEM((8, 256), F32),
        ],
        compiler_params=pltpu.CompilerParams(vmem_limit_bytes=VMEM_BYTES),
        name="network",
    )(counts, image, got, own_target, cut_target, *weights)


def sum_kernel(p_ref, o1_ref, o2_ref, o3_ref, oh_ref,
               from_core, held_core, from_x, held_x, from_z, held_z, from_y, full, send, recv):
    ty = lax.axis_index("ty")
    tx = lax.axis_index("tx")
    core = ty % 2
    x = (ty // 2) % 4
    z = (tx // 4) * 2 + ty // 8
    y = tx % 4

    def device(core_at, x_at, y_at, z_at):
        return ((z_at % 2) * 8 + x_at * 2 + core_at, (z_at // 2) * 4 + y_at)

    def core_peer(d):
        return device(1 - core, x, y, z)

    def x_peer(d):
        return device(core, (x + d) % 4, y, z)

    def y_peer(d):
        return device(core, x, (y + d) % 4, z)

    def z_peer(d):
        return device(core, x, y, (z + d) % 8)

    barrier = pltpu.get_barrier_semaphore()
    for peer, count in ((core_peer, 2), (x_peer, 4), (y_peer, 4), (z_peer, 8)):
        for d in range(1, count):
            pl.semaphore_signal(barrier, inc=1, device_id=peer(d), device_id_type=MESH)
    pl.semaphore_wait(barrier, 14)

    counter = [0]

    def push(src, dst, peer):
        copy = pltpu.make_async_remote_copy(
            src_ref=src, dst_ref=dst, send_sem=send.at[counter[0]], recv_sem=recv.at[counter[0]],
            device_id=peer, device_id_type=MESH)
        counter[0] += 1
        copy.start()
        return copy

    def finish(copies):
        for copy in copies:
            copy.wait()

    def rows(at, count):
        return pl.ds(pl.multiple_of(at, 8), count)

    finish([push(p_ref.at[rows((1 - core) * 768, 768)], from_core, core_peer(1))])
    held_core[...] = p_ref[rows(core * 768, 768), :] + from_core[...]
    finish([push(held_core.at[rows((x + d) % 4 * 192, 192)], from_x.at[d - 1], x_peer(d)) for d in range(1, 4)])
    held_x[...] = held_core[rows(x * 192, 192), :] + from_x[0] + from_x[1] + from_x[2]
    finish([push(held_x.at[rows((z + d) % 8 * 24, 24)], from_z.at[d - 1], z_peer(d)) for d in range(1, 8)])
    total = held_x[rows(z * 24, 24), :]
    for d in range(7):
        total = total + from_z[d]
    held_z[...] = total
    from_y[y] = total
    finish([push(held_z, from_y.at[y], y_peer(d)) for d in range(1, 4)])
    at_z = core * 768 + x * 192 + z * 24
    full[rows(at_z, 24), :] = from_y[0] + from_y[1] + from_y[2] + from_y[3]
    finish([push(full.at[rows(at_z, 24)], full.at[rows(at_z, 24)], z_peer(d)) for d in range(1, 8)])
    at_x = core * 768 + x * 192
    finish([push(full.at[rows(at_x, 192)], full.at[rows(at_x, 192)], x_peer(d)) for d in range(1, 4)])
    at_core = core * 768
    finish([push(full.at[rows(at_core, 768)], full.at[rows(at_core, 768)], core_peer(1))])

    o3_ref[:, :128] = full[0:512, :]
    o3_ref[:, 128:] = full[512:1024, :]
    o2_ref[...] = full[1024:1280, :]
    o1_ref[...] = full[1280:1304, :64]
    oh_ref[:, :128] = full[1304:1312, :]
    oh_ref[:, 128:] = full[1312:1320, :]


def sum_everywhere(packed):
    vmem = pl.BlockSpec(memory_space=pltpu.VMEM)
    return pl.pallas_call(
        sum_kernel,
        out_shape=(
            jax.ShapeDtypeStruct((24, 64), F32),
            jax.ShapeDtypeStruct((256, 128), F32),
            jax.ShapeDtypeStruct((512, 256), F32),
            jax.ShapeDtypeStruct((8, 256), F32),
        ),
        in_specs=[vmem],
        out_specs=(vmem,) * 4,
        scratch_shapes=[
            pltpu.VMEM((768, 128), F32),
            pltpu.VMEM((768, 128), F32),
            pltpu.VMEM((3, 192, 128), F32),
            pltpu.VMEM((192, 128), F32),
            pltpu.VMEM((7, 24, 128), F32),
            pltpu.VMEM((24, 128), F32),
            pltpu.VMEM((4, 24, 128), F32),
            pltpu.VMEM((ROWS, 128), F32),
            pltpu.SemaphoreType.DMA((25,)),
            pltpu.SemaphoreType.DMA((25,)),
        ],
        compiler_params=pltpu.CompilerParams(
            collective_id=1, has_side_effects=True, vmem_limit_bytes=VMEM_BYTES
        ),
        name="sums",
    )(packed)


def per_device(sky_tile, request_offset, request_count, tile_target, cut_target, w_first, w_second, w_third, w_head):
    got = exchange_cutouts(request_offset.reshape(-1), sky_tile)
    packed, cut_pred = network(
        request_count.reshape(-1), sky_tile, got, tile_target[0, 0], cut_target[0, 0],
        (w_first, w_second, w_third, w_head))
    return (*sum_everywhere(packed), cut_pred[None, None])


def solution(mesh):
    return jax.shard_map(
        per_device,
        mesh=mesh,
        in_specs=(
            P(None, "ty", "tx"),
            P("ty", "tx", None, None, None),
            P("ty", "tx", None),
            P("ty", "tx", None, None),
            P("ty", "tx", None, None),
            P(),
            P(),
            P(),
            P(),
        ),
        out_specs=(P(), P(), P(), P(), P("ty", "tx", None, None)),
        check_vma=False,
    )
```

```python
import functools

import jax
import jax.numpy as jnp
from jax import lax
from jax.experimental import pallas as pl
from jax.experimental.pallas import tpu as pltpu
from jax.sharding import PartitionSpec as P

DIRECTIONS = ((-1, -1), (-1, 0), (-1, 1), (0, -1), (0, 1), (1, -1), (1, 0), (1, 1))
MESH = pl.DeviceIdType.MESH
BF = jnp.bfloat16
F32 = jnp.float32
I32 = jnp.int32
VMEM_BYTES = 56 * 1024 * 1024
ROWS = 1536


def iota(shape, dim):
    return lax.broadcasted_iota(I32, shape, dim)


def one_hot(condition, kind=BF):
    return jnp.where(condition, 1.0, 0.0).astype(kind)


def nn(a, b):
    return lax.dot_general(a, b, (((1,), (0,)), ((), ())), preferred_element_type=F32)


def nt(a, b):
    return lax.dot_general(a, b, (((1,), (1,)), ((), ())), preferred_element_type=F32)


def tn(a, b):
    return lax.dot_general(a, b, (((0,), (0,)), ((), ())), preferred_element_type=F32)


def first_mask():
    row = iota((512, 192), 0)
    col = iota((512, 192), 1)
    return ((row >> 7) == ((col & 7) >> 1)) & (((row >> 6) & 1) == jnp.where(col < 96, 0, 1))


def first_spread():
    row = iota((24, 192), 0)
    col = iota((24, 192), 1)
    return row == ((col % 48) // 8) * 4 + (col & 1) * 2 + ((col // 48) & 1)


def silu(pre):
    sig = 0.5 * jnp.tanh(0.5 * pre) + 0.5
    act = pre * sig
    return act.astype(BF), sig + act * (1.0 - sig)


def pick(flag, yes, no):
    return jnp.where(flag, jnp.int32(yes), jnp.int32(no))


def step_of(k):
    at = k + jnp.where(k >= 4, 1, 0)
    return at // 3 - 1, at % 3 - 1


def net_kernel(cnt_ref, off_ref, img_ref, own_target_ref, cut_target_ref, w1_ref, w2_ref, w3_ref, wh_ref,
               grads_ref, cut_pred_ref,
               msg, req, rows_sel, rows_got, cut, got,
               field, place_own, place_cut, wide1, w2, w2t, w3, w3t,
               act1, slope1, act2, slope2, delta1, delta2,
               target, mask, g1, g2, g3, gh,
               req_send, req_recv, rep_send, rep_recv):
    ty = lax.axis_index("ty")
    tx = lax.axis_index("tx")
    n_ty = lax.axis_size("ty")
    n_tx = lax.axis_size("tx")
    upper = (tx % 4) >= 2

    def device(dy, dx):
        return (lax.rem(ty + dy + n_ty, n_ty), lax.rem(tx + dx + n_tx, n_tx))

    barrier = pltpu.get_barrier_semaphore()
    for dy, dx in DIRECTIONS:
        pl.semaphore_signal(barrier, inc=1, device_id=device(dy, dx), device_id_type=MESH)

    lane = iota((8, 128), 1)
    sub = iota((8, 128), 0)
    first = lane < 64
    col_step = 8 * (lane & 7) + ((lane >> 3) & 7)
    row_step = lane & 63

    def offset(coord, p, k):
        return jnp.broadcast_to(off_ref[0, 0, coord, p:p + 1, k:k + 1], (8, 128))

    for k in range(8):
        r0 = jnp.where(first, offset(0, 0, k), offset(0, 1, k))
        c0 = jnp.where(first, offset(1, 0, k), offset(1, 1, k) + 256)
        msg[k] = jnp.where(sub == 0, c0 + col_step, r0 + row_step)

    pl.semaphore_wait(barrier, 8)

    requests = []
    for k, (dy, dx) in enumerate(DIRECTIONS):
        copy = pltpu.make_async_remote_copy(
            src_ref=msg.at[k], dst_ref=req.at[k],
            send_sem=req_send.at[k], recv_sem=req_recv.at[k],
            device_id=device(dy, dx), device_id_type=MESH,
        )
        copy.start()
        requests.append(copy)

    lanes = iota((1024, 128), 1)
    src = iota((1024, 128), 0)
    goal = (src & 7) * 128 + (src >> 8) * 32 + ((src & 255) >> 3)
    for j in range(8):
        place_own[:, j * 128:(j + 1) * 128] = one_hot(lanes + j * 128 == goal)
    src = iota((1024, 128), 0)
    goal = ((src >> 3) & 7) * 128 + ((src >> 6) & 1) * 64 + (src >> 7) * 8 + (src & 7)
    for j in range(8):
        place_cut[:, j * 128:(j + 1) * 128] = one_hot(lanes + j * 128 == goal)

    for copy in requests:
        copy.wait()

    for k in range(8):
        rows_sel[:, k * 128:(k + 1) * 128] = one_hot(iota((128, 128), 0) == req[k][1:2, :])
    for band in range(6):
        rows_got[band] = tn(rows_sel[...], img_ref[band])

    def reply(k):
        dy, dx = step_of(k)
        return pltpu.make_async_remote_copy(
            src_ref=cut.at[k], dst_ref=got.at[k],
            send_sem=rep_send.at[k], recv_sem=rep_recv.at[k],
            device_id=device(-dy, -dx), device_id_type=MESH,
        )

    for k_upper, k_lower in ((0, 2), (3, 4), (5, 7), (2, 0), (4, 3), (7, 5), (1, 1), (6, 6)):
        k = pick(upper, k_upper, k_lower)
        halves = []
        for p in range(2):
            pieces = []
            for block in range(8):
                at = pl.multiple_of(k * 128 + (p * 64 + block * 8), 8)
                for band in range(6):
                    pieces.append(rows_got[band, pl.ds(at, 8), :])
            halves.append(jnp.concatenate(pieces, axis=0).astype(BF))
        cols_sel = one_hot(iota((512, 128), 0) == req[k][0:1, :])
        cut[k] = (nn(halves[0], cols_sel[:256]) + nn(halves[1], cols_sel[256:])).astype(BF)
        reply(k).start()

    up = one_hot((iota((512, 64), 0) & 63) == iota((512, 64), 1))
    wide = nn(nt(up, w1_ref[...]).astype(BF), one_hot(first_spread()))
    wide1[...] = jnp.where(first_mask(), wide, 0.0).astype(BF)
    new = iota((256, 256), 0)
    w2[...] = nn(one_hot(iota((256, 256), 1) == (new & 63) * 4 + (new >> 6)), w2_ref[...]).astype(BF)
    new = iota((256, 256), 1)
    w2t[...] = tn(w2_ref[...], one_hot(iota((256, 256), 0) == (new & 63) * 4 + (new >> 6))).astype(BF)
    new = iota((512, 512), 0)
    w3[...] = nn(one_hot(iota((512, 512), 1) == (new & 127) * 4 + (new >> 7)), w3_ref[...]).astype(BF)
    new = iota((512, 512), 1)
    w3t[...] = tn(w3_ref[...], one_hot(iota((512, 512), 0) == (new & 127) * 4 + (new >> 7))).astype(BF)
    wh = wh_ref[...]

    lines = []
    images = [img_ref[band].astype(F32) for band in range(6)]
    for q in range(4):
        for band in range(6):
            lines.append(jnp.concatenate(
                [images[band][(4 * q + r) * 8:(4 * q + r) * 8 + 8] for r in range(4)], axis=1))
    spread = nn(jnp.concatenate(lines, axis=0).astype(BF), place_own[...]).astype(BF)
    for q in range(4):
        for j in range(8):
            field[j // 4, (j % 4) * 48:(j % 4) * 48 + 48, q * 128:(q + 1) * 128] = (
                spread[q * 48:(q + 1) * 48, j * 128:(j + 1) * 128])

    target[...] = own_target_ref[...]
    mask[...] = jnp.full((8, 512), 1.0, F32)
    g1[...] = jnp.zeros_like(g1)
    g2[...] = jnp.zeros_like(g2)
    g3[...] = jnp.zeros_like(g3)
    gh[...] = jnp.zeros_like(gh)

    def slot_of(step, at):
        early = pick(upper, (0, 3, 5, 1)[at], (2, 4, 7, 1)[at])
        late = pick(upper, (6, 2, 4, 7)[at], (6, 0, 3, 5)[at])
        return jnp.where(step == 1, early, late)

    def part(step, carry):
        @pl.when(step > 0)
        def cutouts():
            stack = []
            for at in range(4):
                k = slot_of(step, at)
                reply(k).wait_recv()
                stack.append(jnp.concatenate([got[k, r * 48:(r + 1) * 48, :] for r in range(8)], axis=1))
                here = slice(at * 128, at * 128 + 128)
                target[:, here] = cut_target_ref[:, pl.ds(pl.multiple_of(k * 128, 128), 128)]
                mask[:, here] = jnp.where((iota((8, 128), 1) >> 6) < cnt_ref[k], 1.0, 0.0)
            spread = nn(jnp.concatenate(stack, axis=0), place_cut[...]).astype(BF)
            for at in range(4):
                for j in range(8):
                    field[j // 4, (j % 4) * 48:(j % 4) * 48 + 48, at * 128:(at + 1) * 128] = (
                        spread[at * 48:(at + 1) * 48, j * 128:(j + 1) * 128])

        for ac in range(2):
            act1[ac], slope1[ac] = silu(nn(wide1[...], field[ac]))
            for ar in range(2):
                at = (ar * 2 + ac) * 128
                act2[at:at + 128], slope2[at:at + 128] = silu(nn(w2t[...], act1[ac, ar * 256:ar * 256 + 256]))
        act3, slope3 = silu(nn(w3t[...], act2[...]))
        pred = nn(wh, act3)
        grad = ((pred - target[...]) * mask[...] * (1.0 / 256.0)).astype(BF)

        @pl.when(step > 0)
        def predictions():
            shown = (pred * mask[...]).astype(BF)
            for at in range(4):
                k = slot_of(step, at)
                cut_pred_ref[:, pl.ds(pl.multiple_of(k * 128, 128), 128)] = shown[:, at * 128:at * 128 + 128]

        gh[...] += nt(grad, act3)
        delta3 = (tn(wh, grad) * slope3).astype(BF)
        g3[...] += nt(act2[...], delta3)
        delta2[...] = (nn(w3[...], delta3) * slope2[...]).astype(BF)
        for ac in range(2):
            for ar in range(2):
                at = (ar * 2 + ac) * 128
                rows = slice(ar * 256, ar * 256 + 256)
                g2[...] += nt(act1[ac, rows], delta2[at:at + 128])
                delta1[ac, rows] = (nn(w2[...], delta2[at:at + 128]) * slope1[ac, rows]).astype(BF)
            g1[...] += nt(delta1[ac], field[ac])
        return carry

    lax.fori_loop(0, 3, part, 0)

    for phase in range(4):
        for half in range(2):
            grads_ref[pl.ds(half * 512 + phase, 128, stride=4), :] = (
                g3[phase * 128:phase * 128 + 128, half * 128:half * 128 + 128])
        grads_ref[pl.ds(1024 + phase, 64, stride=4), :] = g2[phase * 64:phase * 64 + 64, :]
    picked = jnp.where(first_mask(), g1[...], 0.0)
    folded = lax.dot_general(
        one_hot(first_spread(), F32), picked, (((1,), (1,)), ((), ())),
        precision=lax.Precision.HIGHEST, preferred_element_type=F32)
    total = lax.dot_general(
        folded, one_hot((iota((512, 128), 0) & 63) == iota((512, 128), 1), F32), (((1,), (0,)), ((), ())),
        precision=lax.Precision.HIGHEST, preferred_element_type=F32)
    grads_ref[1280:1304, :] = total
    grads_ref[1304:1312, :] = gh[:, :128]
    grads_ref[1312:1320, :] = gh[:, 128:]
    grads_ref[1320:, :] = jnp.zeros((ROWS - 1320, 128), F32)

    for k in range(8):
        reply(jnp.int32(k)).wait_send()


def network(counts, offsets, image, own_target, cut_target, weights):
    vmem = pl.BlockSpec(memory_space=pltpu.VMEM)
    dma = pltpu.SemaphoreType.DMA((8,))
    return pl.pallas_call(
        net_kernel,
        out_shape=(jax.ShapeDtypeStruct((ROWS, 128), F32), jax.ShapeDtypeStruct((8, 1024), BF)),
        in_specs=[pl.BlockSpec(memory_space=pltpu.SMEM)] + [vmem] * 8,
        out_specs=(vmem, vmem),
        scratch_shapes=[
            pltpu.VMEM((8, 8, 128), I32),
            pltpu.VMEM((8, 8, 128), I32),
            pltpu.VMEM((128, 1024), BF),
            pltpu.VMEM((6, 1024, 256), F32),
            pltpu.VMEM((8, 384, 128), BF),
            pltpu.VMEM((8, 384, 128), BF),
            pltpu.VMEM((2, 192, 512), BF),
            pltpu.VMEM((1024, 1024), BF),
            pltpu.VMEM((1024, 1024), BF),
            pltpu.VMEM((512, 192), BF),
            pltpu.VMEM((256, 128), BF),
            pltpu.VMEM((128, 256), BF),
            pltpu.VMEM((512, 256), BF),
            pltpu.VMEM((256, 512), BF),
            pltpu.VMEM((2, 512, 512), BF),
            pltpu.VMEM((2, 512, 512), F32),
            pltpu.VMEM((512, 512), BF),
            pltpu.VMEM((512, 512), F32),
            pltpu.VMEM((2, 512, 512), BF),
            pltpu.VMEM((512, 512), BF),
            pltpu.VMEM((8, 512), F32),
            pltpu.VMEM((8, 512), F32),
            pltpu.VMEM((512, 192), F32),
            pltpu.VMEM((256, 128), F32),
            pltpu.VMEM((512, 256), F32),
            pltpu.VMEM((8, 256), F32),
            dma, dma, dma, dma,
        ],
        compiler_params=pltpu.CompilerParams(
            collective_id=0, has_side_effects=True, vmem_limit_bytes=VMEM_BYTES
        ),
        name="network",
    )(counts, offsets, image, own_target, cut_target, *weights)


def sum_kernel(p_ref, full, from_core, held_core, from_xy, from_z, held_z, send, recv):
    ty = lax.axis_index("ty")
    tx = lax.axis_index("tx")
    core = ty % 2
    x = (ty // 2) % 4
    z = (tx // 4) * 2 + ty // 8
    y = tx % 4
    xy = y * 4 + x

    def device(core_at, xy_at, z_at):
        return ((z_at % 2) * 8 + (xy_at % 4) * 2 + core_at, (z_at // 2) * 4 + xy_at // 4)

    def core_peer():
        return device(1 - core, xy, z)

    def xy_peer(d):
        return ((y + d // 4) % 4) * 4 + (x + d % 4) % 4

    def z_peer(d):
        return device(core, xy, (z + d) % 8)

    barrier = pltpu.get_barrier_semaphore()
    pl.semaphore_signal(barrier, inc=1, device_id=core_peer(), device_id_type=MESH)
    for d in range(1, 16):
        pl.semaphore_signal(barrier, inc=1, device_id=device(core, xy_peer(d), z), device_id_type=MESH)
    for d in range(1, 8):
        pl.semaphore_signal(barrier, inc=1, device_id=z_peer(d), device_id_type=MESH)
    pl.semaphore_wait(barrier, 23)

    counter = [0]

    def push(src, dst, peer):
        copy = pltpu.make_async_remote_copy(
            src_ref=src, dst_ref=dst, send_sem=send.at[counter[0]], recv_sem=recv.at[counter[0]],
            device_id=peer, device_id_type=MESH)
        counter[0] += 1
        copy.start()
        return copy

    def finish(copies):
        for copy in copies:
            copy.wait()

    def rows(at, count):
        return pl.ds(pl.multiple_of(at, 16), count)

    far_first = (10, 2, 8, 6, 9, 11, 14, 1, 3, 4, 12, 5, 7, 13, 15)
    finish([push(p_ref.at[rows((1 - core) * 768, 768)], from_core, core_peer())])
    held_core[...] = p_ref[rows(core * 768, 768), :] + from_core[...]
    finish([push(held_core.at[rows(xy_peer(d) * 48, 48)], from_xy.at[d - 1], device(core, xy_peer(d), z))
            for d in far_first])
    total = held_core[rows(xy * 48, 48), :]
    for d in range(15):
        total = total + from_xy[d]
    held_z[...] = total
    from_z[z] = total
    finish([push(held_z, from_z.at[z], z_peer(d)) for d in (4, 3, 5, 2, 6, 1, 7)])
    total = from_z[0]
    for d in range(1, 8):
        total = total + from_z[d]
    at_xy = core * 768 + xy * 48
    full[rows(at_xy, 48), :] = total
    mine = full.at[rows(at_xy, 48)]
    finish([push(mine, mine, device(core, xy_peer(d), z)) for d in far_first])
    mine = full.at[rows(core * 768, 768)]
    finish([push(mine, mine, core_peer())])


def sum_everywhere(packed):
    vmem = pl.BlockSpec(memory_space=pltpu.VMEM)
    return pl.pallas_call(
        sum_kernel,
        out_shape=jax.ShapeDtypeStruct((ROWS, 128), F32),
        in_specs=[vmem],
        out_specs=vmem,
        scratch_shapes=[
            pltpu.VMEM((768, 128), F32),
            pltpu.VMEM((768, 128), F32),
            pltpu.VMEM((15, 48, 128), F32),
            pltpu.VMEM((8, 48, 128), F32),
            pltpu.VMEM((48, 128), F32),
            pltpu.SemaphoreType.DMA((39,)),
            pltpu.SemaphoreType.DMA((39,)),
        ],
        compiler_params=pltpu.CompilerParams(
            collective_id=1, has_side_effects=True, vmem_limit_bytes=VMEM_BYTES
        ),
        name="sums",
    )(packed)


def unpack_kernel(full, shown, o1_ref, o2_ref, o3_ref, oh_ref, cut_pred_ref):
    o3_ref[:, :128] = full[0:512, :]
    o3_ref[:, 128:] = full[512:1024, :]
    o2_ref[...] = full[1024:1280, :]
    o1_ref[...] = full[1280:1304, :64]
    oh_ref[:, :128] = full[1304:1312, :]
    oh_ref[:, 128:] = full[1312:1320, :]
    cut_pred_ref[...] = shown[...]


def unpack(full, shown):
    vmem = pl.BlockSpec(memory_space=pltpu.VMEM)
    return pl.pallas_call(
        unpack_kernel,
        out_shape=(
            jax.ShapeDtypeStruct((24, 64), F32),
            jax.ShapeDtypeStruct((256, 128), F32),
            jax.ShapeDtypeStruct((512, 256), F32),
            jax.ShapeDtypeStruct((8, 256), F32),
            jax.ShapeDtypeStruct((8, 1024), BF),
        ),
        in_specs=[vmem, vmem],
        out_specs=(vmem,) * 5,
        name="unpack",
    )(full, shown)


def per_device(sky_tile, request_offset, request_count, tile_target, cut_target, w_first, w_second, w_third, w_head):
    packed, cut_pred = network(
        request_count.reshape(-1), request_offset.transpose(0, 1, 3, 4, 2), sky_tile,
        tile_target[0, 0], cut_target[0, 0], (w_first, w_second, w_third, w_head))
    *sums, shown = unpack(sum_everywhere(packed), cut_pred)
    return (*sums, shown[None, None])


def solution(mesh):
    return jax.shard_map(
        per_device,
        mesh=mesh,
        in_specs=(
            P(None, "ty", "tx"),
            P("ty", "tx", None, None, None),
            P("ty", "tx", None),
            P("ty", "tx", None, None),
            P("ty", "tx", None, None),
            P(),
            P(),
            P(),
            P(),
        ),
        out_specs=(P(), P(), P(), P(), P("ty", "tx", None, None)),
        check_vma=False,
    )
```

```python
import functools

import jax
import jax.numpy as jnp
from jax import lax
from jax.experimental import pallas as pl
from jax.experimental.pallas import tpu as pltpu
from jax.sharding import PartitionSpec as P

DIRECTIONS = ((-1, -1), (-1, 0), (-1, 1), (0, -1), (0, 1), (1, -1), (1, 0), (1, 1))
MESH = pl.DeviceIdType.MESH
BF = jnp.bfloat16
F32 = jnp.float32
I32 = jnp.int32
VMEM_BYTES = 56 * 1024 * 1024
ROWS = 1536


def iota(shape, dim):
    return lax.broadcasted_iota(I32, shape, dim)


def one_hot(condition, kind=BF):
    return jnp.where(condition, 1.0, 0.0).astype(kind)


def nn(a, b):
    return lax.dot_general(a, b, (((1,), (0,)), ((), ())), preferred_element_type=F32)


def nt(a, b):
    return lax.dot_general(a, b, (((1,), (1,)), ((), ())), preferred_element_type=F32)


def tn(a, b):
    return lax.dot_general(a, b, (((0,), (0,)), ((), ())), preferred_element_type=F32)


def first_mask():
    row = iota((512, 192), 0)
    col = iota((512, 192), 1)
    return ((row >> 7) == ((col & 7) >> 1)) & (((row >> 6) & 1) == jnp.where(col < 96, 0, 1))


def first_spread():
    row = iota((24, 192), 0)
    col = iota((24, 192), 1)
    return row == ((col % 48) // 8) * 4 + (col & 1) * 2 + ((col // 48) & 1)


def silu(pre):
    sig = 0.5 * jnp.tanh(0.5 * pre) + 0.5
    act = pre * sig
    return act.astype(BF), sig + act * (1.0 - sig)


def pick(flag, yes, no):
    return jnp.where(flag, jnp.int32(yes), jnp.int32(no))


def step_of(k):
    at = k + jnp.where(k >= 4, 1, 0)
    return at // 3 - 1, at % 3 - 1


def net_kernel(cnt_ref, off_ref, img_hbm, own_target_hbm, cut_target_hbm, w1_hbm, w2_hbm, w3_hbm, wh_hbm,
               full, cut_pred_ref,
               img_ref, own_target_ref, cut_target_ref, w1_ref, w2_ref, w3_ref, wh_ref,
               msg, req, rows_sel, rows_got, cut, got,
               field, place_own, place_cut, wide1, w2, w2t, w3, w3t,
               act1, slope1, act2, slope2, delta1, delta2,
               target, mask, g1, g2, g3, gh,
               parts_a, from_core_a, held_core_a, from_xy_a, held_z_a, from_z_a,
               parts_b, from_core_b, held_core_b, from_xy_b, held_z_b, from_z_b,
               fetch, req_send, req_recv, rep_send, rep_recv, sum_send, sum_recv):
    ty = lax.axis_index("ty")
    tx = lax.axis_index("tx")
    n_ty = lax.axis_size("ty")
    n_tx = lax.axis_size("tx")
    core = ty % 2
    x = (ty // 2) % 4
    y = tx % 4
    z = (tx // 4) * 2 + ty // 8
    xy = y * 4 + x
    upper = y >= 2

    def device(dy, dx):
        return (lax.rem(ty + dy + n_ty, n_ty), lax.rem(tx + dx + n_tx, n_tx))

    def place_of(core_at, xy_at, z_at):
        return ((z_at % 2) * 8 + (xy_at % 4) * 2 + core_at, (z_at // 2) * 4 + xy_at // 4)

    def xy_peer(d):
        return ((y + d // 4) % 4) * 4 + (x + d % 4) % 4

    core_peer = place_of(1 - core, xy, z)

    def z_peer(d):
        return place_of(core, xy, (z + d) % 8)

    barrier = pltpu.get_barrier_semaphore()
    greeted = [device(dy, dx) for dy, dx in DIRECTIONS] + [core_peer]
    greeted += [z_peer(d) for d in range(1, 8)]
    greeted += [place_of(core, xy_peer(d), z) for d in range(1, 16)]
    for peer in greeted:
        pl.semaphore_signal(barrier, inc=1, device_id=peer, device_id_type=MESH)

    fetched = []
    for at, (src, dst) in enumerate((
            (img_hbm, img_ref), (w1_hbm, w1_ref), (w2_hbm, w2_ref), (w3_hbm, w3_ref), (wh_hbm, wh_ref),
            (own_target_hbm, own_target_ref), (cut_target_hbm, cut_target_ref))):
        copy = pltpu.make_async_copy(src, dst, fetch.at[at])
        copy.start()
        fetched.append(copy)

    lane = iota((8, 128), 1)
    sub = iota((8, 128), 0)
    first = lane < 64
    col_step = 8 * (lane & 7) + ((lane >> 3) & 7)
    row_step = lane & 63

    def offset(coord, p, k):
        return jnp.broadcast_to(off_ref[0, 0, coord, p:p + 1, k:k + 1], (8, 128))

    for k in range(8):
        r0 = jnp.where(first, offset(0, 0, k), offset(0, 1, k))
        c0 = jnp.where(first, offset(1, 0, k), offset(1, 1, k) + 256)
        msg[k] = jnp.where(sub == 0, c0 + col_step, r0 + row_step)

    pl.semaphore_wait(barrier, len(greeted))

    requests = []
    for k, (dy, dx) in enumerate(DIRECTIONS):
        copy = pltpu.make_async_remote_copy(
            src_ref=msg.at[k], dst_ref=req.at[k],
            send_sem=req_send.at[k], recv_sem=req_recv.at[k],
            device_id=device(dy, dx), device_id_type=MESH,
        )
        copy.start()
        requests.append(copy)

    lanes = iota((1024, 128), 1)
    src = iota((1024, 128), 0)
    goal = (src & 7) * 128 + (src >> 8) * 32 + ((src & 255) >> 3)
    for j in range(8):
        place_own[:, j * 128:(j + 1) * 128] = one_hot(lanes + j * 128 == goal)
    src = iota((1024, 128), 0)
    goal = ((src >> 3) & 7) * 128 + ((src >> 6) & 1) * 64 + (src >> 7) * 8 + (src & 7)
    for j in range(8):
        place_cut[:, j * 128:(j + 1) * 128] = one_hot(lanes + j * 128 == goal)

    fetched[0].wait()
    for copy in requests:
        copy.wait()

    def reply(k):
        dy, dx = step_of(k)
        return pltpu.make_async_remote_copy(
            src_ref=cut.at[k], dst_ref=got.at[k],
            send_sem=rep_send.at[k], recv_sem=rep_recv.at[k],
            device_id=device(-dy, -dx), device_id_type=MESH,
        )

    for group in (((0, 2), (3, 4), (5, 7)), ((2, 0), (4, 3), (7, 5), (1, 1), (6, 6))):
        slots = [pick(upper, *pair) for pair in group]
        wide_rows = 128 * len(slots)
        for at, k in enumerate(slots):
            rows_sel[:, at * 128:(at + 1) * 128] = one_hot(iota((128, 128), 0) == req[k][1:2, :])
        for band in range(6):
            rows_got[band, :wide_rows] = tn(rows_sel[:, :wide_rows], img_ref[band])
        for at, k in enumerate(slots):
            halves = []
            for p in range(2):
                pieces = []
                for block in range(8):
                    row = at * 128 + p * 64 + block * 8
                    for band in range(6):
                        pieces.append(rows_got[band, row:row + 8, :])
                halves.append(jnp.concatenate(pieces, axis=0).astype(BF))
            cols_sel = one_hot(iota((512, 128), 0) == req[k][0:1, :])
            cut[k] = (nn(halves[0], cols_sel[:256]) + nn(halves[1], cols_sel[256:])).astype(BF)
            reply(k).start()

    for copy in fetched[1:]:
        copy.wait()

    up = one_hot((iota((512, 64), 0) & 63) == iota((512, 64), 1))
    wide = nn(nt(up, w1_ref[...]).astype(BF), one_hot(first_spread()))
    wide1[...] = jnp.where(first_mask(), wide, 0.0).astype(BF)
    new = iota((256, 256), 0)
    w2[...] = nn(one_hot(iota((256, 256), 1) == (new & 63) * 4 + (new >> 6)), w2_ref[...]).astype(BF)
    new = iota((256, 256), 1)
    w2t[...] = tn(w2_ref[...], one_hot(iota((256, 256), 0) == (new & 63) * 4 + (new >> 6))).astype(BF)
    new = iota((512, 512), 0)
    w3[...] = nn(one_hot(iota((512, 512), 1) == (new & 127) * 4 + (new >> 7)), w3_ref[...]).astype(BF)
    new = iota((512, 512), 1)
    w3t[...] = tn(w3_ref[...], one_hot(iota((512, 512), 0) == (new & 127) * 4 + (new >> 7))).astype(BF)
    wh = wh_ref[...]

    lines = []
    images = [img_ref[band].astype(F32) for band in range(6)]
    for q in range(4):
        for band in range(6):
            lines.append(jnp.concatenate(
                [images[band][(4 * q + r) * 8:(4 * q + r) * 8 + 8] for r in range(4)], axis=1))
    spread = nn(jnp.concatenate(lines, axis=0).astype(BF), place_own[...]).astype(BF)
    for q in range(4):
        for j in range(8):
            field[j // 4, (j % 4) * 48:(j % 4) * 48 + 48, q * 128:(q + 1) * 128] = (
                spread[q * 48:(q + 1) * 48, j * 128:(j + 1) * 128])

    target[...] = own_target_ref[...]
    mask[...] = jnp.full((8, 512), 1.0, F32)
    g1[...] = jnp.zeros_like(g1)
    g2[...] = jnp.zeros_like(g2)
    g3[...] = jnp.zeros_like(g3)
    gh[...] = jnp.zeros_like(gh)

    def slot_of(step, at):
        early = pick(upper, (0, 3, 5, 1)[at], (2, 4, 7, 1)[at])
        late = pick(upper, (6, 2, 4, 7)[at], (6, 0, 3, 5)[at])
        return jnp.where(step == 1, early, late)

    def take(step):
        stack = []
        for at in range(4):
            k = slot_of(step, at)
            reply(k).wait_recv()
            stack.append(jnp.concatenate([got[k, r * 48:(r + 1) * 48, :] for r in range(8)], axis=1))
            here = slice(at * 128, at * 128 + 128)
            target[:, here] = cut_target_ref[:, pl.ds(pl.multiple_of(k * 128, 128), 128)]
            mask[:, here] = jnp.where((iota((8, 128), 1) >> 6) < cnt_ref[k], 1.0, 0.0)
        spread = nn(jnp.concatenate(stack, axis=0), place_cut[...]).astype(BF)
        for at in range(4):
            for j in range(8):
                field[j // 4, (j % 4) * 48:(j % 4) * 48 + 48, at * 128:(at + 1) * 128] = (
                    spread[at * 48:(at + 1) * 48, j * 128:(j + 1) * 128])

    def show(step, pred):
        shown = (pred * mask[...]).astype(BF)
        for at in range(4):
            k = slot_of(step, at)
            cut_pred_ref[:, pl.ds(pl.multiple_of(k * 128, 128), 128)] = shown[:, at * 128:at * 128 + 128]

    def upward():
        for ac in range(2):
            act1[ac], slope1[ac] = silu(nn(wide1[...], field[ac]))
            for ar in range(2):
                at = (ar * 2 + ac) * 128
                act2[at:at + 128], slope2[at:at + 128] = silu(nn(w2t[...], act1[ac, ar * 256:ar * 256 + 256]))
        act3, slope3 = silu(nn(w3t[...], act2[...]))
        pred = nn(wh, act3)
        grad = ((pred - target[...]) * mask[...] * (1.0 / 256.0)).astype(BF)
        gh[...] += nt(grad, act3)
        delta3 = (tn(wh, grad) * slope3).astype(BF)
        g3[...] += nt(act2[...], delta3)
        return pred, delta3

    def back_third(delta3):
        delta2[...] = (nn(w3[...], delta3) * slope2[...]).astype(BF)

    def back_second(ac):
        for ar in range(2):
            at = (ar * 2 + ac) * 128
            rows = slice(ar * 256, ar * 256 + 256)
            g2[...] += nt(act1[ac, rows], delta2[at:at + 128])
            delta1[ac, rows] = (nn(w2[...], delta2[at:at + 128]) * slope1[ac, rows]).astype(BF)
        g1[...] += nt(delta1[ac], field[ac])

    def part(step, carry):
        @pl.when(step > 0)
        def cutouts():
            take(step)

        pred, delta3 = upward()

        @pl.when(step > 0)
        def predictions():
            show(step, pred)

        back_third(delta3)
        for ac in range(2):
            back_second(ac)
        return carry

    lax.fori_loop(0, 2, part, 0)

    used = [0]

    def push(src, dst, peer):
        copy = pltpu.make_async_remote_copy(
            src_ref=src, dst_ref=dst, send_sem=sum_send.at[used[0]], recv_sem=sum_recv.at[used[0]],
            device_id=peer, device_id_type=MESH)
        used[0] += 1
        copy.start()
        return copy

    def finish(copies):
        for copy in copies:
            copy.wait()

    def rows(at, count):
        return pl.ds(pl.multiple_of(at, 8), count)

    far_first = (10, 2, 8, 6, 9, 11, 14, 1, 3, 4, 12, 5, 7, 13, 15)
    far_z = (4, 3, 5, 2, 6, 1, 7)

    class Stream:
        def __init__(self, base, piece, parts, from_core, held_core, from_xy, held_z, from_z):
            self.base, self.piece, self.half = base, piece, piece * 16
            self.parts, self.from_core, self.held_core = parts, from_core, held_core
            self.from_xy, self.held_z, self.from_z = from_xy, held_z, from_z

        def send_core(self):
            self.going = [push(self.parts.at[rows((1 - core) * self.half, self.half)], self.from_core, core_peer)]

        def send_plane(self):
            finish(self.going)
            self.held_core[...] = self.parts[rows(core * self.half, self.half), :] + self.from_core[...]
            self.going = [
                push(self.held_core.at[rows(xy_peer(d) * self.piece, self.piece)], self.from_xy.at[d - 1],
                     place_of(core, xy_peer(d), z)) for d in far_first]

        def send_z(self):
            finish(self.going)
            total = self.held_core[rows(xy * self.piece, self.piece), :]
            for d in range(15):
                total = total + self.from_xy[d]
            self.held_z[...] = total
            self.from_z[z] = total
            self.going = [push(self.held_z, self.from_z.at[z], z_peer(d)) for d in far_z]

        def gather_plane(self):
            finish(self.going)
            total = self.from_z[0]
            for d in range(1, 8):
                total = total + self.from_z[d]
            at = self.base + core * self.half + xy * self.piece
            full[rows(at, self.piece), :] = total
            mine = full.at[rows(at, self.piece)]
            self.going = [push(mine, mine, place_of(core, xy_peer(d), z)) for d in far_first]

        def gather_core(self):
            finish(self.going)
            mine = full.at[rows(self.base + core * self.half, self.half)]
            self.going = [push(mine, mine, core_peer)]

        def end(self):
            finish(self.going)

    third = Stream(0, 32, parts_a, from_core_a, held_core_a, from_xy_a, held_z_a, from_z_a)
    others = Stream(1024, 16, parts_b, from_core_b, held_core_b, from_xy_b, held_z_b, from_z_b)

    take(2)
    pred, delta3 = upward()
    for phase in range(4):
        for half in range(2):
            parts_a[pl.ds(half * 512 + phase, 128, stride=4), :] = (
                g3[phase * 128:phase * 128 + 128, half * 128:half * 128 + 128])
    third.send_core()
    show(2, pred)
    back_third(delta3)
    back_second(0)
    third.send_plane()
    back_second(1)
    for phase in range(4):
        parts_b[pl.ds(phase, 64, stride=4), :] = g2[phase * 64:phase * 64 + 64, :]
    picked = jnp.where(first_mask(), g1[...], 0.0)
    folded = lax.dot_general(
        one_hot(first_spread(), F32), picked, (((1,), (1,)), ((), ())),
        precision=lax.Precision.HIGHEST, preferred_element_type=F32)
    parts_b[256:280, :] = lax.dot_general(
        folded, one_hot((iota((512, 128), 0) & 63) == iota((512, 128), 1), F32), (((1,), (0,)), ((), ())),
        precision=lax.Precision.HIGHEST, preferred_element_type=F32)
    parts_b[280:288, :] = gh[:, :128]
    parts_b[288:296, :] = gh[:, 128:]
    parts_b[296:, :] = jnp.zeros((216, 128), F32)
    others.send_core()
    third.send_z()
    others.send_plane()
    third.gather_plane()
    others.send_z()
    third.gather_core()
    others.gather_plane()
    others.gather_core()
    third.end()
    others.end()
    for k in range(8):
        reply(jnp.int32(k)).wait_send()


def network(counts, offsets, image, own_target, cut_target, weights):
    vmem = pl.BlockSpec(memory_space=pltpu.VMEM)
    dma = pltpu.SemaphoreType.DMA((8,))
    return pl.pallas_call(
        net_kernel,
        out_shape=(jax.ShapeDtypeStruct((ROWS, 128), F32), jax.ShapeDtypeStruct((8, 1024), BF)),
        in_specs=[pl.BlockSpec(memory_space=pltpu.SMEM), vmem] + [pl.BlockSpec(memory_space=pl.ANY)] * 7,
        out_specs=(vmem, vmem),
        scratch_shapes=[
            pltpu.VMEM((6, 128, 256), BF),
            pltpu.VMEM((8, 512), F32),
            pltpu.VMEM((8, 1024), F32),
            pltpu.VMEM((24, 64), BF),
            pltpu.VMEM((256, 128), BF),
            pltpu.VMEM((512, 256), BF),
            pltpu.VMEM((8, 256), BF),
            pltpu.VMEM((8, 8, 128), I32),
            pltpu.VMEM((8, 8, 128), I32),
            pltpu.VMEM((128, 640), BF),
            pltpu.VMEM((6, 640, 256), F32),
            pltpu.VMEM((8, 384, 128), BF),
            pltpu.VMEM((8, 384, 128), BF),
            pltpu.VMEM((2, 192, 512), BF),
            pltpu.VMEM((1024, 1024), BF),
            pltpu.VMEM((1024, 1024), BF),
            pltpu.VMEM((512, 192), BF),
            pltpu.VMEM((256, 128), BF),
            pltpu.VMEM((128, 256), BF),
            pltpu.VMEM((512, 256), BF),
            pltpu.VMEM((256, 512), BF),
            pltpu.VMEM((2, 512, 512), BF),
            pltpu.VMEM((2, 512, 512), F32),
            pltpu.VMEM((512, 512), BF),
            pltpu.VMEM((512, 512), F32),
            pltpu.VMEM((2, 512, 512), BF),
            pltpu.VMEM((512, 512), BF),
            pltpu.VMEM((8, 512), F32),
            pltpu.VMEM((8, 512), F32),
            pltpu.VMEM((512, 192), F32),
            pltpu.VMEM((256, 128), F32),
            pltpu.VMEM((512, 256), F32),
            pltpu.VMEM((8, 256), F32),
            pltpu.VMEM((1024, 128), F32),
            pltpu.VMEM((512, 128), F32),
            pltpu.VMEM((512, 128), F32),
            pltpu.VMEM((15, 32, 128), F32),
            pltpu.VMEM((32, 128), F32),
            pltpu.VMEM((8, 32, 128), F32),
            pltpu.VMEM((512, 128), F32),
            pltpu.VMEM((256, 128), F32),
            pltpu.VMEM((256, 128), F32),
            pltpu.VMEM((15, 16, 128), F32),
            pltpu.VMEM((16, 128), F32),
            pltpu.VMEM((8, 16, 128), F32),
            dma, dma, dma, dma, dma,
            pltpu.SemaphoreType.DMA((78,)),
            pltpu.SemaphoreType.DMA((78,)),
        ],
        compiler_params=pltpu.CompilerParams(
            collective_id=0, has_side_effects=True, vmem_limit_bytes=VMEM_BYTES
        ),
        name="network",
    )(counts, offsets, image, own_target, cut_target, *weights)


def unpack_kernel(full, shown, o1_ref, o2_ref, o3_ref, oh_ref, cut_pred_ref):
    o3_ref[:, :128] = full[0:512, :]
    o3_ref[:, 128:] = full[512:1024, :]
    o2_ref[...] = full[1024:1280, :]
    o1_ref[...] = full[1280:1304, :64]
    oh_ref[:, :128] = full[1304:1312, :]
    oh_ref[:, 128:] = full[1312:1320, :]
    cut_pred_ref[...] = shown[...]


def unpack(full, shown):
    vmem = pl.BlockSpec(memory_space=pltpu.VMEM)
    return pl.pallas_call(
        unpack_kernel,
        out_shape=(
            jax.ShapeDtypeStruct((24, 64), F32),
            jax.ShapeDtypeStruct((256, 128), F32),
            jax.ShapeDtypeStruct((512, 256), F32),
            jax.ShapeDtypeStruct((8, 256), F32),
            jax.ShapeDtypeStruct((8, 1024), BF),
        ),
        in_specs=[vmem, vmem],
        out_specs=(vmem,) * 5,
        name="unpack",
    )(full, shown)


def per_device(sky_tile, request_offset, request_count, tile_target, cut_target, w_first, w_second, w_third, w_head):
    full, cut_pred = network(
        request_count.reshape(-1), request_offset.transpose(0, 1, 3, 4, 2), sky_tile,
        tile_target[0, 0], cut_target[0, 0], (w_first, w_second, w_third, w_head))
    *sums, shown = unpack(full, cut_pred)
    return (*sums, shown[None, None])


def solution(mesh):
    return jax.shard_map(
        per_device,
        mesh=mesh,
        in_specs=(
            P(None, "ty", "tx"),
            P("ty", "tx", None, None, None),
            P("ty", "tx", None),
            P("ty", "tx", None, None),
            P("ty", "tx", None, None),
            P(),
            P(),
            P(),
            P(),
        ),
        out_specs=(P(), P(), P(), P(), P("ty", "tx", None, None)),
        check_vma=False,
    )
```

```python
import functools

import jax
import jax.numpy as jnp
from jax import lax
from jax.experimental import pallas as pl
from jax.experimental.pallas import tpu as pltpu
from jax.sharding import PartitionSpec as P

DIRECTIONS = ((-1, -1), (-1, 0), (-1, 1), (0, -1), (0, 1), (1, -1), (1, 0), (1, 1))
MESH = pl.DeviceIdType.MESH
BF = jnp.bfloat16
F32 = jnp.float32
I32 = jnp.int32
VMEM_BYTES = 56 * 1024 * 1024
ROWS = 1536


def iota(shape, dim):
    return lax.broadcasted_iota(I32, shape, dim)


def one_hot(condition, kind=BF):
    return jnp.where(condition, 1.0, 0.0).astype(kind)


def nn(a, b):
    return lax.dot_general(a, b, (((1,), (0,)), ((), ())), preferred_element_type=F32)


def nt(a, b):
    return lax.dot_general(a, b, (((1,), (1,)), ((), ())), preferred_element_type=F32)


def tn(a, b):
    return lax.dot_general(a, b, (((0,), (0,)), ((), ())), preferred_element_type=F32)


def first_mask():
    row = iota((512, 192), 0)
    col = iota((512, 192), 1)
    return ((row >> 7) == ((col & 7) >> 1)) & (((row >> 6) & 1) == jnp.where(col < 96, 0, 1))


def first_spread():
    row = iota((24, 192), 0)
    col = iota((24, 192), 1)
    return row == ((col % 48) // 8) * 4 + (col & 1) * 2 + ((col // 48) & 1)


def silu(pre):
    sig = 0.5 * jnp.tanh(0.5 * pre) + 0.5
    act = pre * sig
    return act.astype(BF), sig + act * (1.0 - sig)


def pick(flag, yes, no):
    return jnp.where(flag, jnp.int32(yes), jnp.int32(no))


def step_of(k):
    at = k + jnp.where(k >= 4, 1, 0)
    return at // 3 - 1, at % 3 - 1


def net_kernel(cnt_ref, off_ref, img_hbm, own_target_hbm, cut_target_hbm, w1_hbm, w2_hbm, w3_hbm, wh_hbm,
               full, cut_pred_ref,
               img_ref, own_target_ref, cut_target_ref, w1_ref, w2_ref, w3_ref, wh_ref,
               msg, req, rows_sel, rows_got, cut, got, passing,
               field, place_own, place_cut, wide1, w2, w2t, w3, w3t,
               act1, slope1, act2, slope2, delta1, delta2,
               target, mask, g1, g2, g3, gh,
               parts_a, from_core_a, held_core_a, from_xy_a, held_z_a, from_z_a,
               parts_b, from_core_b, held_core_b, from_xy_b, held_z_b, from_z_b,
               fetch, req_send, req_recv, rep_send, rep_recv, pass_sem, sum_send, sum_recv):
    ty = lax.axis_index("ty")
    tx = lax.axis_index("tx")
    n_ty = lax.axis_size("ty")
    n_tx = lax.axis_size("tx")
    core = ty % 2
    x = (ty // 2) % 4
    y = tx % 4
    z = (tx // 4) * 2 + ty // 8
    xy = y * 4 + x
    upper = y >= 2

    def device(dy, dx):
        return (lax.rem(ty + dy + n_ty, n_ty), lax.rem(tx + dx + n_tx, n_tx))

    def place_of(core_at, xy_at, z_at):
        return ((z_at % 2) * 8 + (xy_at % 4) * 2 + core_at, (z_at // 2) * 4 + xy_at // 4)

    def xy_peer(d):
        return ((y + d // 4) % 4) * 4 + (x + d % 4) % 4

    core_peer = place_of(1 - core, xy, z)

    def z_peer(d):
        return place_of(core, xy, (z + d) % 8)

    barrier = pltpu.get_barrier_semaphore()
    greeted = [device(dy, dx) for dy, dx in DIRECTIONS] + [core_peer]
    greeted += [z_peer(d) for d in range(1, 8)]
    greeted += [place_of(core, xy_peer(d), z) for d in range(1, 16)]
    for peer in greeted:
        pl.semaphore_signal(barrier, inc=1, device_id=peer, device_id_type=MESH)

    fetched = []
    for at, (src, dst) in enumerate((
            (img_hbm, img_ref), (w1_hbm, w1_ref), (w2_hbm, w2_ref), (w3_hbm, w3_ref), (wh_hbm, wh_ref),
            (own_target_hbm, own_target_ref), (cut_target_hbm, cut_target_ref))):
        copy = pltpu.make_async_copy(src, dst, fetch.at[at])
        copy.start()
        fetched.append(copy)

    lane = iota((8, 128), 1)
    sub = iota((8, 128), 0)
    first = lane < 64
    col_step = 8 * (lane & 7) + ((lane >> 3) & 7)
    row_step = lane & 63

    def offset(coord, p, k):
        return jnp.broadcast_to(off_ref[0, 0, coord, p:p + 1, k:k + 1], (8, 128))

    for k in range(8):
        r0 = jnp.where(first, offset(0, 0, k), offset(0, 1, k))
        c0 = jnp.where(first, offset(1, 0, k), offset(1, 1, k) + 256)
        msg[k] = jnp.where(sub == 0, c0 + col_step, r0 + row_step)

    pl.semaphore_wait(barrier, len(greeted))

    requests = []
    for k, (dy, dx) in enumerate(DIRECTIONS):
        copy = pltpu.make_async_remote_copy(
            src_ref=msg.at[k], dst_ref=req.at[k],
            send_sem=req_send.at[k], recv_sem=req_recv.at[k],
            device_id=device(dy, dx), device_id_type=MESH,
        )
        copy.start()
        requests.append(copy)

    lanes = iota((1024, 128), 1)
    src = iota((1024, 128), 0)
    goal = (src & 7) * 128 + (src >> 8) * 32 + ((src & 255) >> 3)
    for j in range(8):
        place_own[:, j * 128:(j + 1) * 128] = one_hot(lanes + j * 128 == goal)
    src = iota((1024, 128), 0)
    goal = ((src >> 3) & 7) * 128 + ((src >> 6) & 1) * 64 + (src >> 7) * 8 + (src & 7)
    for j in range(8):
        place_cut[:, j * 128:(j + 1) * 128] = one_hot(lanes + j * 128 == goal)

    fetched[0].wait()
    for copy in requests:
        copy.wait()

    def reply(k):
        dy, dx = step_of(k)
        return pltpu.make_async_remote_copy(
            src_ref=cut.at[k], dst_ref=got.at[k],
            send_sem=rep_send.at[k], recv_sem=rep_recv.at[k],
            device_id=device(-dy, -dx), device_id_type=MESH,
        )

    at_edge = (y == 0) | (y == 3)
    relayed = ((3, 4), (0, 2))
    by_relay = (at_edge, at_edge & (core == 0))
    relay_tx = lax.rem(tx + pick(y == 3, 13, 3), 16)
    onward_tx = lax.rem(tx + pick(y == 3, 12, 4), 16)

    def to_relay(which):
        return pltpu.make_async_remote_copy(
            src_ref=cut.at[pick(y == 3, *relayed[which])], dst_ref=passing.at[which],
            send_sem=pass_sem.at[which], recv_sem=pass_sem.at[2 + which],
            device_id=(ty, relay_tx), device_id_type=MESH,
        )

    def onward(which):
        slot = pick(y == 0, *relayed[which])
        return pltpu.make_async_remote_copy(
            src_ref=passing.at[which], dst_ref=got.at[slot],
            send_sem=pass_sem.at[4 + which], recv_sem=rep_recv.at[slot],
            device_id=(lax.rem(ty + which, n_ty), onward_tx), device_id_type=MESH,
        )

    for group in (((0, 2), (3, 4), (5, 7)), ((2, 0), (4, 3), (7, 5), (1, 1), (6, 6))):
        slots = [pick(upper, *pair) for pair in group]
        wide_rows = 128 * len(slots)
        for at, k in enumerate(slots):
            rows_sel[:, at * 128:(at + 1) * 128] = one_hot(iota((128, 128), 0) == req[k][1:2, :])
        for band in range(6):
            rows_got[band, :wide_rows] = tn(rows_sel[:, :wide_rows], img_ref[band])
        for at, k in enumerate(slots):
            halves = []
            for p in range(2):
                pieces = []
                for block in range(8):
                    row = at * 128 + p * 64 + block * 8
                    for band in range(6):
                        pieces.append(rows_got[band, row:row + 8, :])
                halves.append(jnp.concatenate(pieces, axis=0).astype(BF))
            cols_sel = one_hot(iota((512, 128), 0) == req[k][0:1, :])
            cut[k] = (nn(halves[0], cols_sel[:256]) + nn(halves[1], cols_sel[256:])).astype(BF)
            if group[at] not in relayed:
                reply(k).start()
                continue

            which = relayed.index(group[at])

            @pl.when(by_relay[which])
            def first_leg():
                to_relay(which).start()

            @pl.when(jnp.logical_not(by_relay[which]))
            def straight():
                reply(k).start()

    for copy in fetched[1:]:
        copy.wait()

    up = one_hot((iota((512, 64), 0) & 63) == iota((512, 64), 1))
    wide = nn(nt(up, w1_ref[...]).astype(BF), one_hot(first_spread()))
    wide1[...] = jnp.where(first_mask(), wide, 0.0).astype(BF)
    new = iota((256, 256), 0)
    w2[...] = nn(one_hot(iota((256, 256), 1) == (new & 63) * 4 + (new >> 6)), w2_ref[...]).astype(BF)
    new = iota((256, 256), 1)
    w2t[...] = tn(w2_ref[...], one_hot(iota((256, 256), 0) == (new & 63) * 4 + (new >> 6))).astype(BF)
    new = iota((512, 512), 0)
    w3[...] = nn(one_hot(iota((512, 512), 1) == (new & 127) * 4 + (new >> 7)), w3_ref[...]).astype(BF)
    new = iota((512, 512), 1)
    w3t[...] = tn(w3_ref[...], one_hot(iota((512, 512), 0) == (new & 127) * 4 + (new >> 7))).astype(BF)
    wh = wh_ref[...]

    lines = []
    images = [img_ref[band].astype(F32) for band in range(6)]
    for q in range(4):
        for band in range(6):
            lines.append(jnp.concatenate(
                [images[band][(4 * q + r) * 8:(4 * q + r) * 8 + 8] for r in range(4)], axis=1))
    spread = nn(jnp.concatenate(lines, axis=0).astype(BF), place_own[...]).astype(BF)
    for q in range(4):
        for j in range(8):
            field[j // 4, (j % 4) * 48:(j % 4) * 48 + 48, q * 128:(q + 1) * 128] = (
                spread[q * 48:(q + 1) * 48, j * 128:(j + 1) * 128])

    target[...] = own_target_ref[...]
    mask[...] = jnp.full((8, 512), 1.0, F32)
    g1[...] = jnp.zeros_like(g1)
    g2[...] = jnp.zeros_like(g2)
    g3[...] = jnp.zeros_like(g3)
    gh[...] = jnp.zeros_like(gh)

    def slot_of(step, at):
        early = pick(upper, (0, 3, 5, 1)[at], (2, 4, 7, 1)[at])
        late = pick(upper, (6, 2, 4, 7)[at], (6, 0, 3, 5)[at])
        return jnp.where(step == 1, early, late)

    def take(step):
        stack = []
        for at in range(4):
            k = slot_of(step, at)
            reply(k).wait_recv()
            stack.append(jnp.concatenate([got[k, r * 48:(r + 1) * 48, :] for r in range(8)], axis=1))
            here = slice(at * 128, at * 128 + 128)
            target[:, here] = cut_target_ref[:, pl.ds(pl.multiple_of(k * 128, 128), 128)]
            mask[:, here] = jnp.where((iota((8, 128), 1) >> 6) < cnt_ref[k], 1.0, 0.0)
        spread = nn(jnp.concatenate(stack, axis=0), place_cut[...]).astype(BF)
        for at in range(4):
            for j in range(8):
                field[j // 4, (j % 4) * 48:(j % 4) * 48 + 48, at * 128:(at + 1) * 128] = (
                    spread[at * 48:(at + 1) * 48, j * 128:(j + 1) * 128])

    def show(step, pred):
        shown = (pred * mask[...]).astype(BF)
        for at in range(4):
            k = slot_of(step, at)
            cut_pred_ref[:, pl.ds(pl.multiple_of(k * 128, 128), 128)] = shown[:, at * 128:at * 128 + 128]

    def upward():
        for ac in range(2):
            act1[ac], slope1[ac] = silu(nn(wide1[...], field[ac]))
            for ar in range(2):
                at = (ar * 2 + ac) * 128
                act2[at:at + 128], slope2[at:at + 128] = silu(nn(w2t[...], act1[ac, ar * 256:ar * 256 + 256]))
        act3, slope3 = silu(nn(w3t[...], act2[...]))
        pred = nn(wh, act3)
        grad = ((pred - target[...]) * mask[...] * (1.0 / 256.0)).astype(BF)
        gh[...] += nt(grad, act3)
        delta3 = (tn(wh, grad) * slope3).astype(BF)
        g3[...] += nt(act2[...], delta3)
        return pred, delta3

    def back_third(delta3):
        delta2[...] = (nn(w3[...], delta3) * slope2[...]).astype(BF)

    def back_second(ac):
        for ar in range(2):
            at = (ar * 2 + ac) * 128
            rows = slice(ar * 256, ar * 256 + 256)
            g2[...] += nt(act1[ac, rows], delta2[at:at + 128])
            delta1[ac, rows] = (nn(w2[...], delta2[at:at + 128]) * slope1[ac, rows]).astype(BF)
        g1[...] += nt(delta1[ac], field[ac])

    def part(step, carry):
        @pl.when(step > 0)
        def cutouts():
            for which in range(2):
                @pl.when(by_relay[which])
                def pass_on():
                    to_relay(which).wait_recv()
                    onward(which).start()

            take(step)

        pred, delta3 = upward()

        @pl.when(step > 0)
        def predictions():
            show(step, pred)

        back_third(delta3)
        for ac in range(2):
            back_second(ac)
        return carry

    lax.fori_loop(0, 2, part, 0)

    used = [0]

    def push(src, dst, peer):
        copy = pltpu.make_async_remote_copy(
            src_ref=src, dst_ref=dst, send_sem=sum_send.at[used[0]], recv_sem=sum_recv.at[used[0]],
            device_id=peer, device_id_type=MESH)
        used[0] += 1
        copy.start()
        return copy

    def finish(copies):
        for copy in copies:
            copy.wait()

    def rows(at, count):
        return pl.ds(pl.multiple_of(at, 8), count)

    far_first = (10, 2, 8, 6, 9, 11, 14, 1, 3, 4, 12, 5, 7, 13, 15)
    far_z = (4, 3, 5, 2, 6, 1, 7)

    class Stream:
        def __init__(self, base, piece, parts, from_core, held_core, from_xy, held_z, from_z):
            self.base, self.piece, self.half = base, piece, piece * 16
            self.parts, self.from_core, self.held_core = parts, from_core, held_core
            self.from_xy, self.held_z, self.from_z = from_xy, held_z, from_z

        def send_core(self):
            self.going = [push(self.parts.at[rows((1 - core) * self.half, self.half)], self.from_core, core_peer)]

        def send_plane(self):
            finish(self.going)
            self.held_core[...] = self.parts[rows(core * self.half, self.half), :] + self.from_core[...]
            self.going = [
                push(self.held_core.at[rows(xy_peer(d) * self.piece, self.piece)], self.from_xy.at[d - 1],
                     place_of(core, xy_peer(d), z)) for d in far_first]

        def send_z(self):
            finish(self.going)
            total = self.held_core[rows(xy * self.piece, self.piece), :]
            for d in range(15):
                total = total + self.from_xy[d]
            self.held_z[...] = total
            self.from_z[z] = total
            self.going = [push(self.held_z, self.from_z.at[z], z_peer(d)) for d in far_z]

        def gather_plane(self):
            finish(self.going)
            total = self.from_z[0]
            for d in range(1, 8):
                total = total + self.from_z[d]
            at = self.base + core * self.half + xy * self.piece
            full[rows(at, self.piece), :] = total
            mine = full.at[rows(at, self.piece)]
            self.going = [push(mine, mine, place_of(core, xy_peer(d), z)) for d in far_first]

        def gather_core(self):
            finish(self.going)
            mine = full.at[rows(self.base + core * self.half, self.half)]
            self.going = [push(mine, mine, core_peer)]

        def end(self):
            finish(self.going)

    third = Stream(0, 32, parts_a, from_core_a, held_core_a, from_xy_a, held_z_a, from_z_a)
    others = Stream(1024, 16, parts_b, from_core_b, held_core_b, from_xy_b, held_z_b, from_z_b)

    take(2)
    pred, delta3 = upward()
    for phase in range(4):
        for half in range(2):
            parts_a[pl.ds(half * 512 + phase, 128, stride=4), :] = (
                g3[phase * 128:phase * 128 + 128, half * 128:half * 128 + 128])
    third.send_core()
    show(2, pred)
    back_third(delta3)
    back_second(0)
    third.send_plane()
    back_second(1)
    for phase in range(4):
        parts_b[pl.ds(phase, 64, stride=4), :] = g2[phase * 64:phase * 64 + 64, :]
    picked = jnp.where(first_mask(), g1[...], 0.0)
    folded = lax.dot_general(
        one_hot(first_spread(), F32), picked, (((1,), (1,)), ((), ())),
        precision=lax.Precision.HIGHEST, preferred_element_type=F32)
    parts_b[256:280, :] = lax.dot_general(
        folded, one_hot((iota((512, 128), 0) & 63) == iota((512, 128), 1), F32), (((1,), (0,)), ((), ())),
        precision=lax.Precision.HIGHEST, preferred_element_type=F32)
    parts_b[280:288, :] = gh[:, :128]
    parts_b[288:296, :] = gh[:, 128:]
    parts_b[296:, :] = jnp.zeros((216, 128), F32)
    others.send_core()
    others.send_plane()
    third.send_z()
    others.send_z()
    third.gather_plane()
    others.gather_plane()
    third.gather_core()
    others.gather_core()
    third.end()
    others.end()
    for which in range(2):
        @pl.when(by_relay[which])
        def passed():
            to_relay(which).wait_send()
            onward(which).wait_send()

    for k in range(8):
        straight = jnp.bool_(True)
        for which in range(2):
            if k in relayed[which]:
                straight = jnp.logical_not(by_relay[which] & (pick(y == 3, *relayed[which]) == k))

        @pl.when(straight)
        def answered():
            reply(jnp.int32(k)).wait_send()


def network(counts, offsets, image, own_target, cut_target, weights):
    vmem = pl.BlockSpec(memory_space=pltpu.VMEM)
    dma = pltpu.SemaphoreType.DMA((8,))
    return pl.pallas_call(
        net_kernel,
        out_shape=(jax.ShapeDtypeStruct((ROWS, 128), F32), jax.ShapeDtypeStruct((8, 1024), BF)),
        in_specs=[pl.BlockSpec(memory_space=pltpu.SMEM), vmem] + [pl.BlockSpec(memory_space=pl.ANY)] * 7,
        out_specs=(vmem, vmem),
        scratch_shapes=[
            pltpu.VMEM((6, 128, 256), BF),
            pltpu.VMEM((8, 512), F32),
            pltpu.VMEM((8, 1024), F32),
            pltpu.VMEM((24, 64), BF),
            pltpu.VMEM((256, 128), BF),
            pltpu.VMEM((512, 256), BF),
            pltpu.VMEM((8, 256), BF),
            pltpu.VMEM((8, 8, 128), I32),
            pltpu.VMEM((8, 8, 128), I32),
            pltpu.VMEM((128, 640), BF),
            pltpu.VMEM((6, 640, 256), F32),
            pltpu.VMEM((8, 384, 128), BF),
            pltpu.VMEM((8, 384, 128), BF),
            pltpu.VMEM((2, 384, 128), BF),
            pltpu.VMEM((2, 192, 512), BF),
            pltpu.VMEM((1024, 1024), BF),
            pltpu.VMEM((1024, 1024), BF),
            pltpu.VMEM((512, 192), BF),
            pltpu.VMEM((256, 128), BF),
            pltpu.VMEM((128, 256), BF),
            pltpu.VMEM((512, 256), BF),
            pltpu.VMEM((256, 512), BF),
            pltpu.VMEM((2, 512, 512), BF),
            pltpu.VMEM((2, 512, 512), F32),
            pltpu.VMEM((512, 512), BF),
            pltpu.VMEM((512, 512), F32),
            pltpu.VMEM((2, 512, 512), BF),
            pltpu.VMEM((512, 512), BF),
            pltpu.VMEM((8, 512), F32),
            pltpu.VMEM((8, 512), F32),
            pltpu.VMEM((512, 192), F32),
            pltpu.VMEM((256, 128), F32),
            pltpu.VMEM((512, 256), F32),
            pltpu.VMEM((8, 256), F32),
            pltpu.VMEM((1024, 128), F32),
            pltpu.VMEM((512, 128), F32),
            pltpu.VMEM((512, 128), F32),
            pltpu.VMEM((15, 32, 128), F32),
            pltpu.VMEM((32, 128), F32),
            pltpu.VMEM((8, 32, 128), F32),
            pltpu.VMEM((512, 128), F32),
            pltpu.VMEM((256, 128), F32),
            pltpu.VMEM((256, 128), F32),
            pltpu.VMEM((15, 16, 128), F32),
            pltpu.VMEM((16, 128), F32),
            pltpu.VMEM((8, 16, 128), F32),
            dma, dma, dma, dma, dma,
            pltpu.SemaphoreType.DMA((6,)),
            pltpu.SemaphoreType.DMA((78,)),
            pltpu.SemaphoreType.DMA((78,)),
        ],
        compiler_params=pltpu.CompilerParams(
            collective_id=0, has_side_effects=True, vmem_limit_bytes=VMEM_BYTES
        ),
        name="network",
    )(counts, offsets, image, own_target, cut_target, *weights)


def unpack_kernel(full, shown, o1_ref, o2_ref, o3_ref, oh_ref, cut_pred_ref):
    o3_ref[:, :128] = full[0:512, :]
    o3_ref[:, 128:] = full[512:1024, :]
    o2_ref[...] = full[1024:1280, :]
    o1_ref[...] = full[1280:1304, :64]
    oh_ref[:, :128] = full[1304:1312, :]
    oh_ref[:, 128:] = full[1312:1320, :]
    cut_pred_ref[...] = shown[...]


def unpack(full, shown):
    vmem = pl.BlockSpec(memory_space=pltpu.VMEM)
    return pl.pallas_call(
        unpack_kernel,
        out_shape=(
            jax.ShapeDtypeStruct((24, 64), F32),
            jax.ShapeDtypeStruct((256, 128), F32),
            jax.ShapeDtypeStruct((512, 256), F32),
            jax.ShapeDtypeStruct((8, 256), F32),
            jax.ShapeDtypeStruct((8, 1024), BF),
        ),
        in_specs=[vmem, vmem],
        out_specs=(vmem,) * 5,
        name="unpack",
    )(full, shown)


def per_device(sky_tile, request_offset, request_count, tile_target, cut_target, w_first, w_second, w_third, w_head):
    full, cut_pred = network(
        request_count.reshape(-1), request_offset.transpose(0, 1, 3, 4, 2), sky_tile,
        tile_target[0, 0], cut_target[0, 0], (w_first, w_second, w_third, w_head))
    *sums, shown = unpack(full, cut_pred)
    return (*sums, shown[None, None])


def solution(mesh):
    return jax.shard_map(
        per_device,
        mesh=mesh,
        in_specs=(
            P(None, "ty", "tx"),
            P("ty", "tx", None, None, None),
            P("ty", "tx", None),
            P("ty", "tx", None, None),
            P("ty", "tx", None, None),
            P(),
            P(),
            P(),
            P(),
        ),
        out_specs=(P(), P(), P(), P(), P("ty", "tx", None, None)),
        check_vma=False,
    )
```

```python
import functools

import jax
import jax.numpy as jnp
from jax import lax
from jax.experimental import pallas as pl
from jax.experimental.pallas import tpu as pltpu
from jax.sharding import PartitionSpec as P

DIRECTIONS = ((-1, -1), (-1, 0), (-1, 1), (0, -1), (0, 1), (1, -1), (1, 0), (1, 1))
MESH = pl.DeviceIdType.MESH
BF = jnp.bfloat16
F32 = jnp.float32
I32 = jnp.int32
VMEM_BYTES = 56 * 1024 * 1024
ROWS = 1536


def iota(shape, dim):
    return lax.broadcasted_iota(I32, shape, dim)


def one_hot(condition, kind=BF):
    return jnp.where(condition, 1.0, 0.0).astype(kind)


def nn(a, b):
    return lax.dot_general(a, b, (((1,), (0,)), ((), ())), preferred_element_type=F32)


def nt(a, b):
    return lax.dot_general(a, b, (((1,), (1,)), ((), ())), preferred_element_type=F32)


def tn(a, b):
    return lax.dot_general(a, b, (((0,), (0,)), ((), ())), preferred_element_type=F32)


def first_mask():
    row = iota((512, 192), 0)
    col = iota((512, 192), 1)
    return ((row >> 7) == ((col & 7) >> 1)) & (((row >> 6) & 1) == jnp.where(col < 96, 0, 1))


def first_spread():
    row = iota((24, 192), 0)
    col = iota((24, 192), 1)
    return row == ((col % 48) // 8) * 4 + (col & 1) * 2 + ((col // 48) & 1)


def silu(pre):
    sig = 0.5 * jnp.tanh(0.5 * pre) + 0.5
    act = pre * sig
    return act.astype(BF), sig + act * (1.0 - sig)


def pick(flag, yes, no):
    return jnp.where(flag, jnp.int32(yes), jnp.int32(no))


def step_of(k):
    at = k + jnp.where(k >= 4, 1, 0)
    return at // 3 - 1, at % 3 - 1


def net_kernel(cnt_ref, off_ref, img_hbm, own_target_hbm, cut_target_hbm, w1_hbm, w2_hbm, w3_hbm, wh_hbm,
               full, cut_pred_ref,
               img_ref, own_target_ref, cut_target_ref, w1_ref, w2_ref, w3_ref, wh_ref,
               msg, req, rows_sel, rows_got, cut, got, passing,
               field, place_own, place_cut, wide1, w2, w2t, w3, w3t,
               act1, slope1, act2, slope2, delta1, delta2,
               target, mask, g1, g2, g3, gh,
               parts_a, from_core_a, held_core_a, from_xy_a, held_z_a, from_z_a,
               parts_b, from_core_b, held_core_b, from_xy_b, held_z_b, from_z_b,
               fetch, req_send, req_recv, rep_send, rep_recv, pass_sem, sum_send, sum_recv):
    ty = lax.axis_index("ty")
    tx = lax.axis_index("tx")
    n_ty = lax.axis_size("ty")
    n_tx = lax.axis_size("tx")
    core = ty % 2
    x = (ty // 2) % 4
    y = tx % 4
    z = (tx // 4) * 2 + ty // 8
    xy = y * 4 + x
    upper = y >= 2

    def device(dy, dx):
        return (lax.rem(ty + dy + n_ty, n_ty), lax.rem(tx + dx + n_tx, n_tx))

    def place_of(core_at, xy_at, z_at):
        return ((z_at % 2) * 8 + (xy_at % 4) * 2 + core_at, (z_at // 2) * 4 + xy_at // 4)

    def xy_peer(d):
        return ((y + d // 4) % 4) * 4 + (x + d % 4) % 4

    core_peer = place_of(1 - core, xy, z)

    def z_peer(d):
        return place_of(core, xy, (z + d) % 8)

    barrier = pltpu.get_barrier_semaphore()
    greeted = [device(dy, dx) for dy, dx in DIRECTIONS] + [core_peer]
    greeted += [z_peer(d) for d in range(1, 8)]
    greeted += [place_of(core, xy_peer(d), z) for d in range(1, 16)]
    for peer in greeted:
        pl.semaphore_signal(barrier, inc=1, device_id=peer, device_id_type=MESH)

    fetched = []
    for at, (src, dst) in enumerate((
            (img_hbm, img_ref), (w1_hbm, w1_ref), (w2_hbm, w2_ref), (w3_hbm, w3_ref), (wh_hbm, wh_ref),
            (own_target_hbm, own_target_ref), (cut_target_hbm, cut_target_ref))):
        copy = pltpu.make_async_copy(src, dst, fetch.at[at])
        copy.start()
        fetched.append(copy)

    lane = iota((8, 128), 1)
    sub = iota((8, 128), 0)
    first = lane < 64
    col_step = 8 * (lane & 7) + ((lane >> 3) & 7)
    row_step = lane & 63

    def offset(coord, p, k):
        return jnp.broadcast_to(off_ref[0, 0, coord, p:p + 1, k:k + 1], (8, 128))

    for k in range(8):
        r0 = jnp.where(first, offset(0, 0, k), offset(0, 1, k))
        c0 = jnp.where(first, offset(1, 0, k), offset(1, 1, k) + 256)
        msg[k] = jnp.where(sub == 0, c0 + col_step, r0 + row_step)

    pl.semaphore_wait(barrier, len(greeted))

    for k, (dy, dx) in enumerate(DIRECTIONS):
        copy = pltpu.make_async_remote_copy(
            src_ref=msg.at[k], dst_ref=req.at[k],
            send_sem=req_send.at[0], recv_sem=req_recv.at[0],
            device_id=device(dy, dx), device_id_type=MESH,
        )
        copy.start()

    lanes = iota((1024, 128), 1)
    src = iota((1024, 128), 0)
    goal = (src & 7) * 128 + (src >> 8) * 32 + ((src & 255) >> 3)
    for j in range(8):
        place_own[:, j * 128:(j + 1) * 128] = one_hot(lanes + j * 128 == goal)
    src = iota((1024, 128), 0)
    goal = ((src >> 3) & 7) * 128 + ((src >> 6) & 1) * 64 + (src >> 7) * 8 + (src & 7)
    for j in range(8):
        place_cut[:, j * 128:(j + 1) * 128] = one_hot(lanes + j * 128 == goal)

    fetched[0].wait()
    pltpu.make_async_copy(msg, req, req_recv.at[0]).wait()
    pltpu.make_async_copy(msg, req, req_send.at[0]).wait()

    def reply(k):
        dy, dx = step_of(k)
        return pltpu.make_async_remote_copy(
            src_ref=cut.at[k], dst_ref=got.at[k],
            send_sem=rep_send.at[k], recv_sem=rep_recv.at[k],
            device_id=device(-dy, -dx), device_id_type=MESH,
        )

    at_edge = (y == 0) | (y == 3)
    relayed = ((3, 4), (0, 2))
    by_relay = (at_edge, at_edge & (core == 0))
    relay_tx = lax.rem(tx + pick(y == 3, 13, 3), 16)
    onward_tx = lax.rem(tx + pick(y == 3, 12, 4), 16)

    def to_relay(which):
        return pltpu.make_async_remote_copy(
            src_ref=cut.at[pick(y == 3, *relayed[which])], dst_ref=passing.at[which],
            send_sem=pass_sem.at[which], recv_sem=pass_sem.at[2 + which],
            device_id=(ty, relay_tx), device_id_type=MESH,
        )

    def onward(which):
        slot = pick(y == 0, *relayed[which])
        return pltpu.make_async_remote_copy(
            src_ref=passing.at[which], dst_ref=got.at[slot],
            send_sem=pass_sem.at[4 + which], recv_sem=rep_recv.at[slot],
            device_id=(lax.rem(ty + which, n_ty), onward_tx), device_id_type=MESH,
        )

    for group in (((0, 2), (3, 4), (5, 7)), ((2, 0), (4, 3), (7, 5), (1, 1), (6, 6))):
        slots = [pick(upper, *pair) for pair in group]
        wide_rows = 128 * len(slots)
        for at, k in enumerate(slots):
            rows_sel[:, at * 128:(at + 1) * 128] = one_hot(iota((128, 128), 0) == req[k][1:2, :])
        for band in range(6):
            rows_got[band, :wide_rows] = tn(rows_sel[:, :wide_rows], img_ref[band])
        for at, k in enumerate(slots):
            halves = []
            for p in range(2):
                pieces = []
                for block in range(8):
                    row = at * 128 + p * 64 + block * 8
                    for band in range(6):
                        pieces.append(rows_got[band, row:row + 8, :])
                halves.append(jnp.concatenate(pieces, axis=0).astype(BF))
            cols_sel = one_hot(iota((512, 128), 0) == req[k][0:1, :])
            cut[k] = (nn(halves[0], cols_sel[:256]) + nn(halves[1], cols_sel[256:])).astype(BF)
            if group[at] not in relayed:
                reply(k).start()
                continue

            which = relayed.index(group[at])

            @pl.when(by_relay[which])
            def first_leg():
                to_relay(which).start()

            @pl.when(jnp.logical_not(by_relay[which]))
            def straight():
                reply(k).start()

    for copy in fetched[1:]:
        copy.wait()

    up = one_hot((iota((512, 64), 0) & 63) == iota((512, 64), 1))
    wide = nn(nt(up, w1_ref[...]).astype(BF), one_hot(first_spread()))
    wide1[...] = jnp.where(first_mask(), wide, 0.0).astype(BF)
    new = iota((256, 256), 0)
    w2[...] = nn(one_hot(iota((256, 256), 1) == (new & 63) * 4 + (new >> 6)), w2_ref[...]).astype(BF)
    new = iota((256, 256), 1)
    w2t[...] = tn(w2_ref[...], one_hot(iota((256, 256), 0) == (new & 63) * 4 + (new >> 6))).astype(BF)
    new = iota((512, 512), 0)
    w3[...] = nn(one_hot(iota((512, 512), 1) == (new & 127) * 4 + (new >> 7)), w3_ref[...]).astype(BF)
    new = iota((512, 512), 1)
    w3t[...] = tn(w3_ref[...], one_hot(iota((512, 512), 0) == (new & 127) * 4 + (new >> 7))).astype(BF)
    wh = wh_ref[...]

    lines = []
    images = [img_ref[band].astype(F32) for band in range(6)]
    for q in range(4):
        for band in range(6):
            lines.append(jnp.concatenate(
                [images[band][(4 * q + r) * 8:(4 * q + r) * 8 + 8] for r in range(4)], axis=1))
    spread = nn(jnp.concatenate(lines, axis=0).astype(BF), place_own[...]).astype(BF)
    for q in range(4):
        for j in range(8):
            field[j // 4, (j % 4) * 48:(j % 4) * 48 + 48, q * 128:(q + 1) * 128] = (
                spread[q * 48:(q + 1) * 48, j * 128:(j + 1) * 128])

    target[...] = own_target_ref[...]
    mask[...] = jnp.full((8, 512), 1.0, F32)
    g1[...] = jnp.zeros_like(g1)
    g2[...] = jnp.zeros_like(g2)
    g3[...] = jnp.zeros_like(g3)
    gh[...] = jnp.zeros_like(gh)

    def slot_of(step, at):
        early = pick(upper, (0, 3, 5, 1)[at], (2, 4, 7, 1)[at])
        late = pick(upper, (6, 2, 4, 7)[at], (6, 0, 3, 5)[at])
        return jnp.where(step == 1, early, late)

    def take(step):
        stack = []
        for at in range(4):
            k = slot_of(step, at)
            reply(k).wait_recv()
            stack.append(jnp.concatenate([got[k, r * 48:(r + 1) * 48, :] for r in range(8)], axis=1))
            here = slice(at * 128, at * 128 + 128)
            target[:, here] = cut_target_ref[:, pl.ds(pl.multiple_of(k * 128, 128), 128)]
            mask[:, here] = jnp.where((iota((8, 128), 1) >> 6) < cnt_ref[k], 1.0, 0.0)
        spread = nn(jnp.concatenate(stack, axis=0), place_cut[...]).astype(BF)
        for at in range(4):
            for j in range(8):
                field[j // 4, (j % 4) * 48:(j % 4) * 48 + 48, at * 128:(at + 1) * 128] = (
                    spread[at * 48:(at + 1) * 48, j * 128:(j + 1) * 128])

    def show(step, pred):
        shown = (pred * mask[...]).astype(BF)
        for at in range(4):
            k = slot_of(step, at)
            cut_pred_ref[:, pl.ds(pl.multiple_of(k * 128, 128), 128)] = shown[:, at * 128:at * 128 + 128]

    def upward():
        for ac in range(2):
            act1[ac], slope1[ac] = silu(nn(wide1[...], field[ac]))
            for ar in range(2):
                at = (ar * 2 + ac) * 128
                act2[at:at + 128], slope2[at:at + 128] = silu(nn(w2t[...], act1[ac, ar * 256:ar * 256 + 256]))
        act3, slope3 = silu(nn(w3t[...], act2[...]))
        pred = nn(wh, act3)
        grad = ((pred - target[...]) * mask[...] * (1.0 / 256.0)).astype(BF)
        gh[...] += nt(grad, act3)
        delta3 = (tn(wh, grad) * slope3).astype(BF)
        g3[...] += nt(act2[...], delta3)
        return pred, delta3

    def back_third(delta3):
        delta2[...] = (nn(w3[...], delta3) * slope2[...]).astype(BF)

    def back_second(ac):
        for ar in range(2):
            at = (ar * 2 + ac) * 128
            rows = slice(ar * 256, ar * 256 + 256)
            g2[...] += nt(act1[ac, rows], delta2[at:at + 128])
            delta1[ac, rows] = (nn(w2[...], delta2[at:at + 128]) * slope1[ac, rows]).astype(BF)
        g1[...] += nt(delta1[ac], field[ac])

    def part(step, carry):
        @pl.when(step > 0)
        def cutouts():
            for which in range(2):
                @pl.when(by_relay[which])
                def pass_on():
                    to_relay(which).wait_recv()
                    onward(which).start()

            take(step)

        pred, delta3 = upward()

        @pl.when(step > 0)
        def predictions():
            show(step, pred)

        back_third(delta3)
        for ac in range(2):
            back_second(ac)
        return carry

    lax.fori_loop(0, 2, part, 0)

    def push(at, src, dst, peer):
        pltpu.make_async_remote_copy(
            src_ref=src, dst_ref=dst, send_sem=sum_send.at[at], recv_sem=sum_recv.at[at],
            device_id=peer, device_id_type=MESH).start()

    def finish(at, alike):
        pltpu.make_async_copy(alike, alike, sum_recv.at[at]).wait()
        pltpu.make_async_copy(alike, alike, sum_send.at[at]).wait()

    def rows(at, count):
        return pl.ds(pl.multiple_of(at, 8), count)

    far_first = (10, 2, 8, 6, 9, 11, 14, 1, 3, 4, 12, 5, 7, 13, 15)
    far_z = (4, 3, 5, 2, 6, 1, 7)

    class Stream:
        def __init__(self, first, base, piece, parts, from_core, held_core, from_xy, held_z, from_z):
            self.first, self.base, self.piece, self.half = first, base, piece, piece * 16
            self.parts, self.from_core, self.held_core = parts, from_core, held_core
            self.from_xy, self.held_z, self.from_z = from_xy, held_z, from_z

        def send_core(self):
            push(self.first, self.parts.at[rows((1 - core) * self.half, self.half)], self.from_core, core_peer)

        def send_plane(self):
            finish(self.first, self.from_core)
            self.held_core[...] = self.parts[rows(core * self.half, self.half), :] + self.from_core[...]
            for d in far_first:
                push(self.first + 1, self.held_core.at[rows(xy_peer(d) * self.piece, self.piece)],
                     self.from_xy.at[d - 1], place_of(core, xy_peer(d), z))

        def send_z(self):
            finish(self.first + 1, self.from_xy)
            total = self.held_core[rows(xy * self.piece, self.piece), :]
            for d in range(15):
                total = total + self.from_xy[d]
            self.held_z[...] = total
            self.from_z[z] = total
            for d in far_z:
                push(self.first + 2, self.held_z, self.from_z.at[z], z_peer(d))

        def gather_plane(self):
            finish(self.first + 2, self.from_z.at[0:7])
            total = self.from_z[0]
            for d in range(1, 8):
                total = total + self.from_z[d]
            mine = full.at[rows(self.base + core * self.half + xy * self.piece, self.piece)]
            mine[...] = total
            for d in far_first:
                push(self.first + 3, mine, mine, place_of(core, xy_peer(d), z))

        def gather_core(self):
            finish(self.first + 3, self.from_xy)
            mine = full.at[rows(self.base + core * self.half, self.half)]
            push(self.first + 4, mine, mine, core_peer)

        def end(self):
            finish(self.first + 4, self.from_core)

    third = Stream(0, 0, 32, parts_a, from_core_a, held_core_a, from_xy_a, held_z_a, from_z_a)
    others = Stream(5, 1024, 16, parts_b, from_core_b, held_core_b, from_xy_b, held_z_b, from_z_b)

    take(2)
    pred, delta3 = upward()
    for phase in range(4):
        for half in range(2):
            parts_a[pl.ds(half * 512 + phase, 128, stride=4), :] = (
                g3[phase * 128:phase * 128 + 128, half * 128:half * 128 + 128])
    third.send_core()
    show(2, pred)
    back_third(delta3)
    back_second(0)
    third.send_plane()
    back_second(1)
    for phase in range(4):
        parts_b[pl.ds(phase, 64, stride=4), :] = g2[phase * 64:phase * 64 + 64, :]
    picked = jnp.where(first_mask(), g1[...], 0.0)
    folded = lax.dot_general(
        one_hot(first_spread(), F32), picked, (((1,), (1,)), ((), ())),
        precision=lax.Precision.HIGHEST, preferred_element_type=F32)
    parts_b[256:280, :] = lax.dot_general(
        folded, one_hot((iota((512, 128), 0) & 63) == iota((512, 128), 1), F32), (((1,), (0,)), ((), ())),
        precision=lax.Precision.HIGHEST, preferred_element_type=F32)
    parts_b[280:288, :] = gh[:, :128]
    parts_b[288:296, :] = gh[:, 128:]
    parts_b[296:, :] = jnp.zeros((216, 128), F32)
    others.send_core()
    others.send_plane()
    third.send_z()
    others.send_z()
    third.gather_plane()
    others.gather_plane()
    third.gather_core()
    others.gather_core()
    third.end()
    others.end()
    for which in range(2):
        @pl.when(by_relay[which])
        def passed():
            to_relay(which).wait_send()
            onward(which).wait_send()

    for k in range(8):
        straight = jnp.bool_(True)
        for which in range(2):
            if k in relayed[which]:
                straight = jnp.logical_not(by_relay[which] & (pick(y == 3, *relayed[which]) == k))

        @pl.when(straight)
        def answered():
            reply(jnp.int32(k)).wait_send()


def network(counts, offsets, image, own_target, cut_target, weights):
    vmem = pl.BlockSpec(memory_space=pltpu.VMEM)
    dma = pltpu.SemaphoreType.DMA((8,))
    return pl.pallas_call(
        net_kernel,
        out_shape=(jax.ShapeDtypeStruct((ROWS, 128), F32), jax.ShapeDtypeStruct((8, 1024), BF)),
        in_specs=[pl.BlockSpec(memory_space=pltpu.SMEM), vmem] + [pl.BlockSpec(memory_space=pl.ANY)] * 7,
        out_specs=(vmem, vmem),
        scratch_shapes=[
            pltpu.VMEM((6, 128, 256), BF),
            pltpu.VMEM((8, 512), F32),
            pltpu.VMEM((8, 1024), F32),
            pltpu.VMEM((24, 64), BF),
            pltpu.VMEM((256, 128), BF),
            pltpu.VMEM((512, 256), BF),
            pltpu.VMEM((8, 256), BF),
            pltpu.VMEM((8, 8, 128), I32),
            pltpu.VMEM((8, 8, 128), I32),
            pltpu.VMEM((128, 640), BF),
            pltpu.VMEM((6, 640, 256), F32),
            pltpu.VMEM((8, 384, 128), BF),
            pltpu.VMEM((8, 384, 128), BF),
            pltpu.VMEM((2, 384, 128), BF),
            pltpu.VMEM((2, 192, 512), BF),
            pltpu.VMEM((1024, 1024), BF),
            pltpu.VMEM((1024, 1024), BF),
            pltpu.VMEM((512, 192), BF),
            pltpu.VMEM((256, 128), BF),
            pltpu.VMEM((128, 256), BF),
            pltpu.VMEM((512, 256), BF),
            pltpu.VMEM((256, 512), BF),
            pltpu.VMEM((2, 512, 512), BF),
            pltpu.VMEM((2, 512, 512), F32),
            pltpu.VMEM((512, 512), BF),
            pltpu.VMEM((512, 512), F32),
            pltpu.VMEM((2, 512, 512), BF),
            pltpu.VMEM((512, 512), BF),
            pltpu.VMEM((8, 512), F32),
            pltpu.VMEM((8, 512), F32),
            pltpu.VMEM((512, 192), F32),
            pltpu.VMEM((256, 128), F32),
            pltpu.VMEM((512, 256), F32),
            pltpu.VMEM((8, 256), F32),
            pltpu.VMEM((1024, 128), F32),
            pltpu.VMEM((512, 128), F32),
            pltpu.VMEM((512, 128), F32),
            pltpu.VMEM((15, 32, 128), F32),
            pltpu.VMEM((32, 128), F32),
            pltpu.VMEM((8, 32, 128), F32),
            pltpu.VMEM((512, 128), F32),
            pltpu.VMEM((256, 128), F32),
            pltpu.VMEM((256, 128), F32),
            pltpu.VMEM((15, 16, 128), F32),
            pltpu.VMEM((16, 128), F32),
            pltpu.VMEM((8, 16, 128), F32),
            dma, dma, dma, dma, dma,
            pltpu.SemaphoreType.DMA((6,)),
            pltpu.SemaphoreType.DMA((10,)),
            pltpu.SemaphoreType.DMA((10,)),
        ],
        compiler_params=pltpu.CompilerParams(
            collective_id=0, has_side_effects=True, vmem_limit_bytes=VMEM_BYTES
        ),
        name="network",
    )(counts, offsets, image, own_target, cut_target, *weights)


def unpack_kernel(full, shown, o1_ref, o2_ref, o3_ref, oh_ref, cut_pred_ref):
    o3_ref[:, :128] = full[0:512, :]
    o3_ref[:, 128:] = full[512:1024, :]
    o2_ref[...] = full[1024:1280, :]
    o1_ref[...] = full[1280:1304, :64]
    oh_ref[:, :128] = full[1304:1312, :]
    oh_ref[:, 128:] = full[1312:1320, :]
    cut_pred_ref[...] = shown[...]


def unpack(full, shown):
    vmem = pl.BlockSpec(memory_space=pltpu.VMEM)
    return pl.pallas_call(
        unpack_kernel,
        out_shape=(
            jax.ShapeDtypeStruct((24, 64), F32),
            jax.ShapeDtypeStruct((256, 128), F32),
            jax.ShapeDtypeStruct((512, 256), F32),
            jax.ShapeDtypeStruct((8, 256), F32),
            jax.ShapeDtypeStruct((8, 1024), BF),
        ),
        in_specs=[vmem, vmem],
        out_specs=(vmem,) * 5,
        name="unpack",
    )(full, shown)


def per_device(sky_tile, request_offset, request_count, tile_target, cut_target, w_first, w_second, w_third, w_head):
    full, cut_pred = network(
        request_count.reshape(-1), request_offset.transpose(0, 1, 3, 4, 2), sky_tile,
        tile_target[0, 0], cut_target[0, 0], (w_first, w_second, w_third, w_head))
    *sums, shown = unpack(full, cut_pred)
    return (*sums, shown[None, None])


def solution(mesh):
    return jax.shard_map(
        per_device,
        mesh=mesh,
        in_specs=(
            P(None, "ty", "tx"),
            P("ty", "tx", None, None, None),
            P("ty", "tx", None),
            P("ty", "tx", None, None),
            P("ty", "tx", None, None),
            P(),
            P(),
            P(),
            P(),
        ),
        out_specs=(P(), P(), P(), P(), P("ty", "tx", None, None)),
        check_vma=False,
    )
```

```python
import functools

import jax
import jax.numpy as jnp
from jax import lax
from jax.experimental import pallas as pl
from jax.experimental.pallas import tpu as pltpu
from jax.sharding import PartitionSpec as P

DIRECTIONS = ((-1, -1), (-1, 0), (-1, 1), (0, -1), (0, 1), (1, -1), (1, 0), (1, 1))
MESH = pl.DeviceIdType.MESH
BF = jnp.bfloat16
F32 = jnp.float32
I32 = jnp.int32
VMEM_BYTES = 56 * 1024 * 1024
ROWS = 1536


def iota(shape, dim):
    return lax.broadcasted_iota(I32, shape, dim)


def one_hot(condition, kind=BF):
    return jnp.where(condition, 1.0, 0.0).astype(kind)


def nn(a, b):
    return lax.dot_general(a, b, (((1,), (0,)), ((), ())), preferred_element_type=F32)


def nt(a, b):
    return lax.dot_general(a, b, (((1,), (1,)), ((), ())), preferred_element_type=F32)


def tn(a, b):
    return lax.dot_general(a, b, (((0,), (0,)), ((), ())), preferred_element_type=F32)


def first_mask():
    row = iota((512, 192), 0)
    col = iota((512, 192), 1)
    return ((row >> 7) == ((col & 7) >> 1)) & (((row >> 6) & 1) == jnp.where(col < 96, 0, 1))


def first_spread():
    row = iota((24, 192), 0)
    col = iota((24, 192), 1)
    return row == ((col % 48) // 8) * 4 + (col & 1) * 2 + ((col // 48) & 1)


def silu(pre):
    sig = 0.5 * jnp.tanh(0.5 * pre) + 0.5
    act = pre * sig
    return act.astype(BF), sig + act * (1.0 - sig)


def pick(flag, yes, no):
    return jnp.where(flag, jnp.int32(yes), jnp.int32(no))


def step_of(k):
    at = k + jnp.where(k >= 4, 1, 0)
    return at // 3 - 1, at % 3 - 1


def net_kernel(cnt_ref, off_ref, img_hbm, own_target_hbm, cut_target_hbm, w1_hbm, w2_hbm, w3_hbm, wh_hbm,
               full, cut_pred_ref,
               img_ref, own_target_ref, cut_target_ref, w1_ref, w2_ref, w3_ref, wh_ref,
               msg, req, rows_sel, rows_got, cut, got, passing,
               field, place_own, place_cut, wide1, w2, w2t, w3, w3t,
               act1, slope1, act2, slope2, delta1, delta2,
               target, mask, g1, g2, g3, gh,
               parts_a, from_core_a, held_core_a, from_xy_a, held_z_a, from_z_a,
               parts_b, from_core_b, held_core_b, from_xy_b, held_z_b, from_z_b,
               fetch, req_send, req_recv, rep_send, rep_recv, pass_sem, sum_send, sum_recv):
    ty = lax.axis_index("ty")
    tx = lax.axis_index("tx")
    n_ty = lax.axis_size("ty")
    n_tx = lax.axis_size("tx")
    core = ty % 2
    x = (ty // 2) % 4
    y = tx % 4
    z = (tx // 4) * 2 + ty // 8
    xy = y * 4 + x
    upper = y >= 2

    def device(dy, dx):
        return (lax.rem(ty + dy + n_ty, n_ty), lax.rem(tx + dx + n_tx, n_tx))

    def place_of(core_at, xy_at, z_at):
        return ((z_at % 2) * 8 + (xy_at % 4) * 2 + core_at, (z_at // 2) * 4 + xy_at // 4)

    def xy_peer(d):
        return ((y + d // 4) % 4) * 4 + (x + d % 4) % 4

    core_peer = place_of(1 - core, xy, z)

    def z_peer(d):
        return place_of(core, xy, (z + d) % 8)

    barrier = pltpu.get_barrier_semaphore()
    greeted = [device(dy, dx) for dy, dx in DIRECTIONS] + [core_peer]
    greeted += [z_peer(d) for d in range(1, 8)]
    greeted += [place_of(core, xy_peer(d), z) for d in range(1, 16)]
    for peer in greeted:
        pl.semaphore_signal(barrier, inc=1, device_id=peer, device_id_type=MESH)

    fetched = []
    for at, (src, dst) in enumerate((
            (img_hbm, img_ref), (w1_hbm, w1_ref), (w2_hbm, w2_ref), (w3_hbm, w3_ref), (wh_hbm, wh_ref),
            (own_target_hbm, own_target_ref), (cut_target_hbm, cut_target_ref))):
        copy = pltpu.make_async_copy(src, dst, fetch.at[at])
        copy.start()
        fetched.append(copy)

    lane = iota((8, 128), 1)
    sub = iota((8, 128), 0)
    first = lane < 64
    col_step = 8 * (lane & 7) + ((lane >> 3) & 7)
    row_step = lane & 63

    def offset(coord, p, k):
        return jnp.broadcast_to(off_ref[0, 0, coord, p:p + 1, k:k + 1], (8, 128))

    for k in range(8):
        r0 = jnp.where(first, offset(0, 0, k), offset(0, 1, k))
        c0 = jnp.where(first, offset(1, 0, k), offset(1, 1, k) + 256)
        msg[k] = jnp.where(sub == 0, c0 + col_step, r0 + row_step)

    pl.semaphore_wait(barrier, len(greeted))

    for k, (dy, dx) in enumerate(DIRECTIONS):
        copy = pltpu.make_async_remote_copy(
            src_ref=msg.at[k], dst_ref=req.at[k],
            send_sem=req_send.at[0], recv_sem=req_recv.at[0],
            device_id=device(dy, dx), device_id_type=MESH,
        )
        copy.start()

    lanes = iota((1024, 128), 1)
    src = iota((1024, 128), 0)
    goal = (src & 7) * 128 + (src >> 8) * 32 + ((src & 255) >> 3)
    for j in range(8):
        place_own[:, j * 128:(j + 1) * 128] = one_hot(lanes + j * 128 == goal)
    src = iota((1024, 128), 0)
    goal = ((src >> 3) & 7) * 128 + ((src >> 6) & 1) * 64 + (src >> 7) * 8 + (src & 7)
    for j in range(8):
        place_cut[:, j * 128:(j + 1) * 128] = one_hot(lanes + j * 128 == goal)

    fetched[0].wait()
    pltpu.make_async_copy(msg, req, req_recv.at[0]).wait()
    pltpu.make_async_copy(msg, req, req_send.at[0]).wait()

    def reply(k):
        dy, dx = step_of(k)
        return pltpu.make_async_remote_copy(
            src_ref=cut.at[k], dst_ref=got.at[k],
            send_sem=rep_send.at[k], recv_sem=rep_recv.at[k],
            device_id=device(-dy, -dx), device_id_type=MESH,
        )

    at_edge = (y == 0) | (y == 3)
    relayed = ((3, 4), (0, 2))
    by_relay = (at_edge, at_edge & (core == 0))
    relay_tx = lax.rem(tx + pick(y == 3, 13, 3), 16)
    onward_tx = lax.rem(tx + pick(y == 3, 12, 4), 16)

    def to_relay(which):
        return pltpu.make_async_remote_copy(
            src_ref=cut.at[pick(y == 3, *relayed[which])], dst_ref=passing.at[which],
            send_sem=pass_sem.at[which], recv_sem=pass_sem.at[2 + which],
            device_id=(ty, relay_tx), device_id_type=MESH,
        )

    def onward(which):
        slot = pick(y == 0, *relayed[which])
        return pltpu.make_async_remote_copy(
            src_ref=passing.at[which], dst_ref=got.at[slot],
            send_sem=pass_sem.at[4 + which], recv_sem=rep_recv.at[slot],
            device_id=(lax.rem(ty + which, n_ty), onward_tx), device_id_type=MESH,
        )

    for group in (((0, 2), (3, 4), (5, 7)), ((2, 0), (4, 3), (7, 5), (1, 1), (6, 6))):
        slots = [pick(upper, *pair) for pair in group]
        wide_rows = 128 * len(slots)
        for at, k in enumerate(slots):
            rows_sel[:, at * 128:(at + 1) * 128] = one_hot(iota((128, 128), 0) == req[k][1:2, :])
        for band in range(6):
            rows_got[band, :wide_rows] = tn(rows_sel[:, :wide_rows], img_ref[band])
        for at, k in enumerate(slots):
            halves = []
            for p in range(2):
                pieces = []
                for block in range(8):
                    row = at * 128 + p * 64 + block * 8
                    for band in range(6):
                        pieces.append(rows_got[band, row:row + 8, :])
                halves.append(jnp.concatenate(pieces, axis=0).astype(BF))
            cols_sel = one_hot(iota((512, 128), 0) == req[k][0:1, :])
            cut[k] = (nn(halves[0], cols_sel[:256]) + nn(halves[1], cols_sel[256:])).astype(BF)
            if group[at] not in relayed:
                reply(k).start()
                continue

            which = relayed.index(group[at])

            @pl.when(by_relay[which])
            def first_leg():
                to_relay(which).start()

            @pl.when(jnp.logical_not(by_relay[which]))
            def straight():
                reply(k).start()

    for copy in fetched[1:]:
        copy.wait()

    up = one_hot((iota((512, 64), 0) & 63) == iota((512, 64), 1))
    wide = nn(nt(up, w1_ref[...]).astype(BF), one_hot(first_spread()))
    wide1[...] = jnp.where(first_mask(), wide, 0.0).astype(BF)
    new = iota((256, 256), 0)
    w2[...] = nn(one_hot(iota((256, 256), 1) == (new & 63) * 4 + (new >> 6)), w2_ref[...]).astype(BF)
    new = iota((256, 256), 1)
    w2t[...] = tn(w2_ref[...], one_hot(iota((256, 256), 0) == (new & 63) * 4 + (new >> 6))).astype(BF)
    new = iota((512, 512), 0)
    w3[...] = nn(one_hot(iota((512, 512), 1) == (new & 127) * 4 + (new >> 7)), w3_ref[...]).astype(BF)
    new = iota((512, 512), 1)
    w3t[...] = tn(w3_ref[...], one_hot(iota((512, 512), 0) == (new & 127) * 4 + (new >> 7))).astype(BF)
    wh = wh_ref[...]

    lines = []
    images = [img_ref[band].astype(F32) for band in range(6)]
    for q in range(4):
        for band in range(6):
            lines.append(jnp.concatenate(
                [images[band][(4 * q + r) * 8:(4 * q + r) * 8 + 8] for r in range(4)], axis=1))
    spread = nn(jnp.concatenate(lines, axis=0).astype(BF), place_own[...]).astype(BF)
    for q in range(4):
        for j in range(8):
            field[j // 4, (j % 4) * 48:(j % 4) * 48 + 48, q * 128:(q + 1) * 128] = (
                spread[q * 48:(q + 1) * 48, j * 128:(j + 1) * 128])

    target[...] = own_target_ref[...]
    mask[...] = jnp.full((8, 512), 1.0, F32)
    g1[...] = jnp.zeros_like(g1)
    g2[...] = jnp.zeros_like(g2)
    g3[...] = jnp.zeros_like(g3)
    gh[...] = jnp.zeros_like(gh)

    def slot_of(step, at):
        early = pick(upper, (0, 3, 5, 1)[at], (2, 4, 7, 1)[at])
        late = pick(upper, (6, 2, 4, 7)[at], (6, 0, 3, 5)[at])
        return jnp.where(step == 1, early, late)

    def take(step):
        stack = []
        for at in range(4):
            k = slot_of(step, at)
            reply(k).wait_recv()
            stack.append(jnp.concatenate([got[k, r * 48:(r + 1) * 48, :] for r in range(8)], axis=1))
            here = slice(at * 128, at * 128 + 128)
            target[:, here] = cut_target_ref[:, pl.ds(pl.multiple_of(k * 128, 128), 128)]
            mask[:, here] = jnp.where((iota((8, 128), 1) >> 6) < cnt_ref[k], 1.0, 0.0)
        spread = nn(jnp.concatenate(stack, axis=0), place_cut[...]).astype(BF)
        for at in range(4):
            for j in range(8):
                field[j // 4, (j % 4) * 48:(j % 4) * 48 + 48, at * 128:(at + 1) * 128] = (
                    spread[at * 48:(at + 1) * 48, j * 128:(j + 1) * 128])

    def show(step, pred):
        shown = (pred * mask[...]).astype(BF)
        for at in range(4):
            k = slot_of(step, at)
            cut_pred_ref[:, pl.ds(pl.multiple_of(k * 128, 128), 128)] = shown[:, at * 128:at * 128 + 128]

    def upward():
        for ac in range(2):
            act1[ac], slope1[ac] = silu(nn(wide1[...], field[ac]))
            for ar in range(2):
                at = (ar * 2 + ac) * 128
                act2[at:at + 128], slope2[at:at + 128] = silu(nn(w2t[...], act1[ac, ar * 256:ar * 256 + 256]))
        act3, slope3 = silu(nn(w3t[...], act2[...]))
        pred = nn(wh, act3)
        grad = ((pred - target[...]) * mask[...] * (1.0 / 256.0)).astype(BF)
        gh[...] += nt(grad, act3)
        delta3 = (tn(wh, grad) * slope3).astype(BF)
        g3[...] += nt(act2[...], delta3)
        return pred, delta3

    def back_third(delta3):
        delta2[...] = (nn(w3[...], delta3) * slope2[...]).astype(BF)

    def back_second(ac):
        for ar in range(2):
            at = (ar * 2 + ac) * 128
            rows = slice(ar * 256, ar * 256 + 256)
            g2[...] += nt(act1[ac, rows], delta2[at:at + 128])
            delta1[ac, rows] = (nn(w2[...], delta2[at:at + 128]) * slope1[ac, rows]).astype(BF)
        g1[...] += nt(delta1[ac], field[ac])

    def part(step, carry):
        @pl.when(step > 0)
        def cutouts():
            take(step)

        pred, delta3 = upward()

        @pl.when(step > 0)
        def predictions():
            show(step, pred)

        for which in range(2):
            @pl.when((step == 0) & by_relay[which])
            def pass_on():
                to_relay(which).wait_recv()
                onward(which).start()

        back_third(delta3)
        for ac in range(2):
            back_second(ac)
        return carry

    lax.fori_loop(0, 2, part, 0)

    def push(at, src, dst, peer):
        pltpu.make_async_remote_copy(
            src_ref=src, dst_ref=dst, send_sem=sum_send.at[at], recv_sem=sum_recv.at[at],
            device_id=peer, device_id_type=MESH).start()

    def finish(at, alike):
        pltpu.make_async_copy(alike, alike, sum_recv.at[at]).wait()
        pltpu.make_async_copy(alike, alike, sum_send.at[at]).wait()

    def rows(at, count):
        return pl.ds(pl.multiple_of(at, 8), count)

    far_first = (10, 6, 9, 14, 11, 2, 8, 5, 15, 7, 13, 1, 4, 3, 12)
    far_z = (4, 3, 5, 2, 6, 1, 7)

    class Stream:
        def __init__(self, first, base, piece, parts, from_core, held_core, from_xy, held_z, from_z):
            self.first, self.base, self.piece, self.half = first, base, piece, piece * 16
            self.parts, self.from_core, self.held_core = parts, from_core, held_core
            self.from_xy, self.held_z, self.from_z = from_xy, held_z, from_z

        def send_core(self):
            push(self.first, self.parts.at[rows((1 - core) * self.half, self.half)], self.from_core, core_peer)

        def send_plane(self):
            finish(self.first, self.from_core)
            self.held_core[...] = self.parts[rows(core * self.half, self.half), :] + self.from_core[...]
            for d in far_first:
                push(self.first + 1, self.held_core.at[rows(xy_peer(d) * self.piece, self.piece)],
                     self.from_xy.at[d - 1], place_of(core, xy_peer(d), z))

        def send_z(self):
            finish(self.first + 1, self.from_xy)
            total = self.held_core[rows(xy * self.piece, self.piece), :]
            for d in range(15):
                total = total + self.from_xy[d]
            self.held_z[...] = total
            self.from_z[z] = total
            for d in far_z:
                push(self.first + 2, self.held_z, self.from_z.at[z], z_peer(d))

        def gather_plane(self):
            finish(self.first + 2, self.from_z.at[0:7])
            total = self.from_z[0]
            for d in range(1, 8):
                total = total + self.from_z[d]
            mine = full.at[rows(self.base + core * self.half + xy * self.piece, self.piece)]
            mine[...] = total
            for d in far_first:
                push(self.first + 3, mine, mine, place_of(core, xy_peer(d), z))

        def gather_core(self):
            finish(self.first + 3, self.from_xy)
            mine = full.at[rows(self.base + core * self.half, self.half)]
            push(self.first + 4, mine, mine, core_peer)

        def end(self):
            finish(self.first + 4, self.from_core)

    third = Stream(0, 0, 32, parts_a, from_core_a, held_core_a, from_xy_a, held_z_a, from_z_a)
    others = Stream(5, 1024, 16, parts_b, from_core_b, held_core_b, from_xy_b, held_z_b, from_z_b)

    take(2)
    pred, delta3 = upward()
    for phase in range(4):
        for half in range(2):
            parts_a[pl.ds(half * 512 + phase, 128, stride=4), :] = (
                g3[phase * 128:phase * 128 + 128, half * 128:half * 128 + 128])
    third.send_core()
    show(2, pred)
    back_third(delta3)
    back_second(0)
    third.send_plane()
    back_second(1)
    for phase in range(4):
        parts_b[pl.ds(phase, 64, stride=4), :] = g2[phase * 64:phase * 64 + 64, :]
    picked = jnp.where(first_mask(), g1[...], 0.0)
    folded = lax.dot_general(
        one_hot(first_spread(), F32), picked, (((1,), (1,)), ((), ())),
        precision=lax.Precision.HIGHEST, preferred_element_type=F32)
    parts_b[256:280, :] = folded[:, :128] + folded[:, 128:256] + folded[:, 256:384] + folded[:, 384:]
    parts_b[280:288, :] = gh[:, :128]
    parts_b[288:296, :] = gh[:, 128:]
    parts_b[296:, :] = jnp.zeros((216, 128), F32)
    others.send_core()
    others.send_plane()
    third.send_z()
    others.send_z()
    third.gather_plane()
    others.gather_plane()
    third.gather_core()
    others.gather_core()
    third.end()
    others.end()
    for which in range(2):
        @pl.when(by_relay[which])
        def passed():
            to_relay(which).wait_send()
            onward(which).wait_send()

    for k in range(8):
        straight = jnp.bool_(True)
        for which in range(2):
            if k in relayed[which]:
                straight = jnp.logical_not(by_relay[which] & (pick(y == 3, *relayed[which]) == k))

        @pl.when(straight)
        def answered():
            reply(jnp.int32(k)).wait_send()


def network(counts, offsets, image, own_target, cut_target, weights):
    vmem = pl.BlockSpec(memory_space=pltpu.VMEM)
    dma = pltpu.SemaphoreType.DMA((8,))
    return pl.pallas_call(
        net_kernel,
        out_shape=(jax.ShapeDtypeStruct((ROWS, 128), F32), jax.ShapeDtypeStruct((8, 1024), BF)),
        in_specs=[pl.BlockSpec(memory_space=pltpu.SMEM), vmem] + [pl.BlockSpec(memory_space=pl.ANY)] * 7,
        out_specs=(vmem, vmem),
        scratch_shapes=[
            pltpu.VMEM((6, 128, 256), BF),
            pltpu.VMEM((8, 512), F32),
            pltpu.VMEM((8, 1024), F32),
            pltpu.VMEM((24, 64), BF),
            pltpu.VMEM((256, 128), BF),
            pltpu.VMEM((512, 256), BF),
            pltpu.VMEM((8, 256), BF),
            pltpu.VMEM((8, 8, 128), I32),
            pltpu.VMEM((8, 8, 128), I32),
            pltpu.VMEM((128, 640), BF),
            pltpu.VMEM((6, 640, 256), F32),
            pltpu.VMEM((8, 384, 128), BF),
            pltpu.VMEM((8, 384, 128), BF),
            pltpu.VMEM((2, 384, 128), BF),
            pltpu.VMEM((2, 192, 512), BF),
            pltpu.VMEM((1024, 1024), BF),
            pltpu.VMEM((1024, 1024), BF),
            pltpu.VMEM((512, 192), BF),
            pltpu.VMEM((256, 128), BF),
            pltpu.VMEM((128, 256), BF),
            pltpu.VMEM((512, 256), BF),
            pltpu.VMEM((256, 512), BF),
            pltpu.VMEM((2, 512, 512), BF),
            pltpu.VMEM((2, 512, 512), F32),
            pltpu.VMEM((512, 512), BF),
            pltpu.VMEM((512, 512), F32),
            pltpu.VMEM((2, 512, 512), BF),
            pltpu.VMEM((512, 512), BF),
            pltpu.VMEM((8, 512), F32),
            pltpu.VMEM((8, 512), F32),
            pltpu.VMEM((512, 192), F32),
            pltpu.VMEM((256, 128), F32),
            pltpu.VMEM((512, 256), F32),
            pltpu.VMEM((8, 256), F32),
            pltpu.VMEM((1024, 128), F32),
            pltpu.VMEM((512, 128), F32),
            pltpu.VMEM((512, 128), F32),
            pltpu.VMEM((15, 32, 128), F32),
            pltpu.VMEM((32, 128), F32),
            pltpu.VMEM((8, 32, 128), F32),
            pltpu.VMEM((512, 128), F32),
            pltpu.VMEM((256, 128), F32),
            pltpu.VMEM((256, 128), F32),
            pltpu.VMEM((15, 16, 128), F32),
            pltpu.VMEM((16, 128), F32),
            pltpu.VMEM((8, 16, 128), F32),
            dma, dma, dma, dma, dma,
            pltpu.SemaphoreType.DMA((6,)),
            pltpu.SemaphoreType.DMA((10,)),
            pltpu.SemaphoreType.DMA((10,)),
        ],
        compiler_params=pltpu.CompilerParams(
            collective_id=0, has_side_effects=True, vmem_limit_bytes=VMEM_BYTES
        ),
        name="network",
    )(counts, offsets, image, own_target, cut_target, *weights)


def unpack_kernel(full, shown, o1_ref, o2_ref, o3_ref, oh_ref, cut_pred_ref):
    o3_ref[:, :128] = full[0:512, :]
    o3_ref[:, 128:] = full[512:1024, :]
    o2_ref[...] = full[1024:1280, :]
    first = full[1280:1304, :]
    o1_ref[...] = first[:, :64] + first[:, 64:]
    oh_ref[:, :128] = full[1304:1312, :]
    oh_ref[:, 128:] = full[1312:1320, :]
    cut_pred_ref[...] = shown[...]


def unpack(full, shown):
    vmem = pl.BlockSpec(memory_space=pltpu.VMEM)
    return pl.pallas_call(
        unpack_kernel,
        out_shape=(
            jax.ShapeDtypeStruct((24, 64), F32),
            jax.ShapeDtypeStruct((256, 128), F32),
            jax.ShapeDtypeStruct((512, 256), F32),
            jax.ShapeDtypeStruct((8, 256), F32),
            jax.ShapeDtypeStruct((8, 1024), BF),
        ),
        in_specs=[vmem, vmem],
        out_specs=(vmem,) * 5,
        name="unpack",
    )(full, shown)


def per_device(sky_tile, request_offset, request_count, tile_target, cut_target, w_first, w_second, w_third, w_head):
    full, cut_pred = network(
        request_count.reshape(-1), request_offset.transpose(0, 1, 3, 4, 2), sky_tile,
        tile_target[0, 0], cut_target[0, 0], (w_first, w_second, w_third, w_head))
    *sums, shown = unpack(full, cut_pred)
    return (*sums, shown[None, None])


def solution(mesh):
    return jax.shard_map(
        per_device,
        mesh=mesh,
        in_specs=(
            P(None, "ty", "tx"),
            P("ty", "tx", None, None, None),
            P("ty", "tx", None),
            P("ty", "tx", None, None),
            P("ty", "tx", None, None),
            P(),
            P(),
            P(),
            P(),
        ),
        out_specs=(P(), P(), P(), P(), P("ty", "tx", None, None)),
        check_vma=False,
    )
```

```python
import functools

import jax
import jax.numpy as jnp
from jax import lax
from jax.experimental import pallas as pl
from jax.experimental.pallas import tpu as pltpu
from jax.sharding import PartitionSpec as P

DIRECTIONS = ((-1, -1), (-1, 0), (-1, 1), (0, -1), (0, 1), (1, -1), (1, 0), (1, 1))
MESH = pl.DeviceIdType.MESH
BF = jnp.bfloat16
F32 = jnp.float32
I32 = jnp.int32
VMEM_BYTES = 56 * 1024 * 1024
ROWS = 1536


def iota(shape, dim):
    return lax.broadcasted_iota(I32, shape, dim)


def one_hot(condition, kind=BF):
    return jnp.where(condition, 1.0, 0.0).astype(kind)


def nn(a, b):
    return lax.dot_general(a, b, (((1,), (0,)), ((), ())), preferred_element_type=F32)


def nt(a, b):
    return lax.dot_general(a, b, (((1,), (1,)), ((), ())), preferred_element_type=F32)


def tn(a, b):
    return lax.dot_general(a, b, (((0,), (0,)), ((), ())), preferred_element_type=F32)


def first_mask():
    row = iota((512, 192), 0)
    col = iota((512, 192), 1)
    return ((row >> 7) == ((col & 7) >> 1)) & (((row >> 6) & 1) == jnp.where(col < 96, 0, 1))


def first_spread():
    row = iota((24, 192), 0)
    col = iota((24, 192), 1)
    return row == ((col % 48) // 8) * 4 + (col & 1) * 2 + ((col // 48) & 1)


def silu(pre):
    sig = 0.5 * jnp.tanh(0.5 * pre) + 0.5
    act = pre * sig
    return act.astype(BF), sig + act * (1.0 - sig)


def pick(flag, yes, no):
    return jnp.where(flag, jnp.int32(yes), jnp.int32(no))


def step_of(k):
    at = k + jnp.where(k >= 4, 1, 0)
    return at // 3 - 1, at % 3 - 1


def net_kernel(cnt_ref, off_ref, img_hbm, own_target_hbm, cut_target_hbm, w1_hbm, w2_hbm, w3_hbm, wh_hbm,
               full, cut_pred_ref,
               img_ref, own_target_ref, cut_target_ref, w1_ref, w2_ref, w3_ref, wh_ref,
               msg, req, rows_sel, rows_got, cut, got, passing,
               field, place_own, place_cut, wide1, w2, w2t, w3, w3t,
               act1, slope1, act2, slope2, delta1, delta2,
               target, mask, g1, g2, g3, gh,
               parts_a, from_core_a, held_core_a, from_xy_a, held_z_a, from_z_a,
               parts_b, from_core_b, held_core_b, from_xy_b, held_z_b, from_z_b,
               fetch, req_send, req_recv, rep_send, rep_recv, pass_sem, sum_send, sum_recv):
    ty = lax.axis_index("ty")
    tx = lax.axis_index("tx")
    n_ty = lax.axis_size("ty")
    n_tx = lax.axis_size("tx")
    core = ty % 2
    x = (ty // 2) % 4
    y = tx % 4
    z = (tx // 4) * 2 + ty // 8
    xy = y * 4 + x
    upper = y >= 2

    def device(dy, dx):
        return (lax.rem(ty + dy + n_ty, n_ty), lax.rem(tx + dx + n_tx, n_tx))

    def place_of(core_at, xy_at, z_at):
        return ((z_at % 2) * 8 + (xy_at % 4) * 2 + core_at, (z_at // 2) * 4 + xy_at // 4)

    def xy_peer(d):
        return ((y + d // 4) % 4) * 4 + (x + d % 4) % 4

    core_peer = place_of(1 - core, xy, z)

    def z_peer(d):
        return place_of(core, xy, (z + d) % 8)

    barrier = pltpu.get_barrier_semaphore()
    greeted = [device(dy, dx) for dy, dx in DIRECTIONS] + [core_peer]
    greeted += [z_peer(d) for d in range(1, 8)]
    greeted += [place_of(core, xy_peer(d), z) for d in range(1, 16)]
    for peer in greeted:
        pl.semaphore_signal(barrier, inc=1, device_id=peer, device_id_type=MESH)

    fetched = []
    for at, (src, dst) in enumerate((
            (img_hbm, img_ref), (w1_hbm, w1_ref), (w2_hbm, w2_ref), (w3_hbm, w3_ref), (wh_hbm, wh_ref),
            (own_target_hbm, own_target_ref), (cut_target_hbm, cut_target_ref))):
        copy = pltpu.make_async_copy(src, dst, fetch.at[at])
        copy.start()
        fetched.append(copy)

    lane = iota((8, 128), 1)
    sub = iota((8, 128), 0)
    first = lane < 64
    col_step = 8 * (lane & 7) + ((lane >> 3) & 7)
    row_step = lane & 63

    def offset(coord, p, k):
        return jnp.broadcast_to(off_ref[0, 0, coord, p:p + 1, k:k + 1], (8, 128))

    for k in range(8):
        r0 = jnp.where(first, offset(0, 0, k), offset(0, 1, k))
        c0 = jnp.where(first, offset(1, 0, k), offset(1, 1, k) + 256)
        msg[k] = jnp.where(sub == 0, c0 + col_step, r0 + row_step)

    pl.semaphore_wait(barrier, len(greeted))

    for k, (dy, dx) in enumerate(DIRECTIONS):
        copy = pltpu.make_async_remote_copy(
            src_ref=msg.at[k], dst_ref=req.at[k],
            send_sem=req_send.at[0], recv_sem=req_recv.at[0],
            device_id=device(dy, dx), device_id_type=MESH,
        )
        copy.start()

    lanes = iota((1024, 128), 1)
    src = iota((1024, 128), 0)
    goal = (src & 7) * 128 + (src >> 8) * 32 + ((src & 255) >> 3)
    for j in range(8):
        place_own[:, j * 128:(j + 1) * 128] = one_hot(lanes + j * 128 == goal)
    src = iota((1024, 128), 0)
    goal = ((src >> 3) & 7) * 128 + ((src >> 6) & 1) * 64 + (src >> 7) * 8 + (src & 7)
    for j in range(8):
        place_cut[:, j * 128:(j + 1) * 128] = one_hot(lanes + j * 128 == goal)

    fetched[0].wait()
    pltpu.make_async_copy(msg, req, req_recv.at[0]).wait()
    pltpu.make_async_copy(msg, req, req_send.at[0]).wait()

    def reply(k):
        dy, dx = step_of(k)
        return pltpu.make_async_remote_copy(
            src_ref=cut.at[k], dst_ref=got.at[k],
            send_sem=rep_send.at[k], recv_sem=rep_recv.at[k],
            device_id=device(-dy, -dx), device_id_type=MESH,
        )

    at_edge = (y == 0) | (y == 3)
    relayed = ((3, 4), (0, 2))
    by_relay = (at_edge, at_edge & (core == 0))
    relay_tx = lax.rem(tx + pick(y == 3, 13, 3), 16)
    onward_tx = lax.rem(tx + pick(y == 3, 12, 4), 16)

    def to_relay(which):
        return pltpu.make_async_remote_copy(
            src_ref=cut.at[pick(y == 3, *relayed[which])], dst_ref=passing.at[which],
            send_sem=pass_sem.at[which], recv_sem=pass_sem.at[2 + which],
            device_id=(ty, relay_tx), device_id_type=MESH,
        )

    def onward(which):
        slot = pick(y == 0, *relayed[which])
        return pltpu.make_async_remote_copy(
            src_ref=passing.at[which], dst_ref=got.at[slot],
            send_sem=pass_sem.at[4 + which], recv_sem=rep_recv.at[slot],
            device_id=(lax.rem(ty + which, n_ty), onward_tx), device_id_type=MESH,
        )

    for group in (((0, 2), (3, 4), (5, 7)), ((2, 0), (4, 3), (7, 5), (1, 1), (6, 6))):
        slots = [pick(upper, *pair) for pair in group]
        wide_rows = 128 * len(slots)
        for at, k in enumerate(slots):
            rows_sel[:, at * 128:(at + 1) * 128] = one_hot(iota((128, 128), 0) == req[k][1:2, :])
        for band in range(6):
            rows_got[band, :wide_rows] = tn(rows_sel[:, :wide_rows], img_ref[band])
        for at, k in enumerate(slots):
            halves = []
            for p in range(2):
                pieces = []
                for block in range(8):
                    row = at * 128 + p * 64 + block * 8
                    for band in range(6):
                        pieces.append(rows_got[band, row:row + 8, :])
                halves.append(jnp.concatenate(pieces, axis=0).astype(BF))
            cols_sel = one_hot(iota((512, 128), 0) == req[k][0:1, :])
            cut[k] = (nn(halves[0], cols_sel[:256]) + nn(halves[1], cols_sel[256:])).astype(BF)
            if group[at] not in relayed:
                reply(k).start()
                continue

            which = relayed.index(group[at])

            @pl.when(by_relay[which])
            def first_leg():
                to_relay(which).start()

            @pl.when(jnp.logical_not(by_relay[which]))
            def straight():
                reply(k).start()

    for copy in fetched[1:]:
        copy.wait()

    up = one_hot((iota((512, 64), 0) & 63) == iota((512, 64), 1))
    wide = nn(nt(up, w1_ref[...]).astype(BF), one_hot(first_spread()))
    wide1[...] = jnp.where(first_mask(), wide, 0.0).astype(BF)
    new = iota((256, 256), 0)
    w2[...] = nn(one_hot(iota((256, 256), 1) == (new & 63) * 4 + (new >> 6)), w2_ref[...]).astype(BF)
    new = iota((256, 256), 1)
    w2t[...] = tn(w2_ref[...], one_hot(iota((256, 256), 0) == (new & 63) * 4 + (new >> 6))).astype(BF)
    new = iota((512, 512), 0)
    w3[...] = nn(one_hot(iota((512, 512), 1) == (new & 127) * 4 + (new >> 7)), w3_ref[...]).astype(BF)
    new = iota((512, 512), 1)
    w3t[...] = tn(w3_ref[...], one_hot(iota((512, 512), 0) == (new & 127) * 4 + (new >> 7))).astype(BF)
    wh = wh_ref[...]

    lines = []
    images = [img_ref[band].astype(F32) for band in range(6)]
    for q in range(4):
        for band in range(6):
            lines.append(jnp.concatenate(
                [images[band][(4 * q + r) * 8:(4 * q + r) * 8 + 8] for r in range(4)], axis=1))
    spread = nn(jnp.concatenate(lines, axis=0).astype(BF), place_own[...]).astype(BF)
    for q in range(4):
        for j in range(8):
            field[j // 4, (j % 4) * 48:(j % 4) * 48 + 48, q * 128:(q + 1) * 128] = (
                spread[q * 48:(q + 1) * 48, j * 128:(j + 1) * 128])

    target[...] = own_target_ref[...]
    mask[...] = jnp.full((8, 512), 1.0, F32)
    g1[...] = jnp.zeros_like(g1)
    g2[...] = jnp.zeros_like(g2)
    g3[...] = jnp.zeros_like(g3)
    gh[...] = jnp.zeros_like(gh)

    def slot_of(step, at):
        early = pick(upper, (0, 3, 5, 1)[at], (2, 4, 7, 1)[at])
        late = pick(upper, (6, 2, 4, 7)[at], (6, 0, 3, 5)[at])
        return jnp.where(step == 1, early, late)

    def take(step):
        stack = []
        for at in range(4):
            k = slot_of(step, at)
            reply(k).wait_recv()
            stack.append(jnp.concatenate([got[k, r * 48:(r + 1) * 48, :] for r in range(8)], axis=1))
            here = slice(at * 128, at * 128 + 128)
            target[:, here] = cut_target_ref[:, pl.ds(pl.multiple_of(k * 128, 128), 128)]
            mask[:, here] = jnp.where((iota((8, 128), 1) >> 6) < cnt_ref[k], 1.0, 0.0)
        spread = nn(jnp.concatenate(stack, axis=0), place_cut[...]).astype(BF)
        for at in range(4):
            for j in range(8):
                field[j // 4, (j % 4) * 48:(j % 4) * 48 + 48, at * 128:(at + 1) * 128] = (
                    spread[at * 48:(at + 1) * 48, j * 128:(j + 1) * 128])

    def show(step, pred):
        shown = (pred * mask[...]).astype(BF)
        for at in range(4):
            k = slot_of(step, at)
            cut_pred_ref[:, pl.ds(pl.multiple_of(k * 128, 128), 128)] = shown[:, at * 128:at * 128 + 128]

    def upward():
        for ac in range(2):
            act1[ac], slope1[ac] = silu(nn(wide1[...], field[ac]))
            for ar in range(2):
                at = (ar * 2 + ac) * 128
                act2[at:at + 128], slope2[at:at + 128] = silu(nn(w2t[...], act1[ac, ar * 256:ar * 256 + 256]))
        act3, slope3 = silu(nn(w3t[...], act2[...]))
        pred = nn(wh, act3)
        grad = ((pred - target[...]) * mask[...] * (1.0 / 256.0)).astype(BF)
        gh[...] += nt(grad, act3)
        delta3 = (tn(wh, grad) * slope3).astype(BF)
        g3[...] += nt(act2[...], delta3)
        return pred, delta3

    def back_third(delta3):
        delta2[...] = (nn(w3[...], delta3) * slope2[...]).astype(BF)

    def back_second(ac):
        for ar in range(2):
            at = (ar * 2 + ac) * 128
            rows = slice(ar * 256, ar * 256 + 256)
            g2[...] += nt(act1[ac, rows], delta2[at:at + 128])
            delta1[ac, rows] = (nn(w2[...], delta2[at:at + 128]) * slope1[ac, rows]).astype(BF)
        g1[...] += nt(delta1[ac], field[ac])

    def part(step, carry):
        @pl.when(step > 0)
        def cutouts():
            take(step)

        pred, delta3 = upward()

        @pl.when(step > 0)
        def predictions():
            show(step, pred)

        for which in range(2):
            @pl.when((step == 0) & by_relay[which])
            def pass_on():
                to_relay(which).wait_recv()
                onward(which).start()

        back_third(delta3)
        for ac in range(2):
            back_second(ac)
        return carry

    lax.fori_loop(0, 2, part, 0)

    def push(at, src, dst, peer):
        pltpu.make_async_remote_copy(
            src_ref=src, dst_ref=dst, send_sem=sum_send.at[at], recv_sem=sum_recv.at[at],
            device_id=peer, device_id_type=MESH).start()

    def finish(at, alike):
        pltpu.make_async_copy(alike, alike, sum_recv.at[at]).wait()
        pltpu.make_async_copy(alike, alike, sum_send.at[at]).wait()

    def rows(at, count):
        return pl.ds(pl.multiple_of(at, 8), count)

    far_first = (10, 6, 9, 14, 11, 2, 8, 5, 15, 7, 13, 1, 4, 3, 12)
    far_z = (4, 3, 5, 2, 6, 1, 7)

    class Stream:
        def __init__(self, first, base, piece, parts, from_core, held_core, from_xy, held_z, from_z):
            self.first, self.base, self.piece, self.half = first, base, piece, piece * 16
            self.parts, self.from_core, self.held_core = parts, from_core, held_core
            self.from_xy, self.held_z, self.from_z = from_xy, held_z, from_z

        def send_core(self):
            push(self.first, self.parts.at[rows((1 - core) * self.half, self.half)], self.from_core, core_peer)

        def send_plane(self):
            finish(self.first, self.from_core)
            self.held_core[...] = self.parts[rows(core * self.half, self.half), :] + self.from_core[...]
            for d in far_first:
                push(self.first + 1, self.held_core.at[rows(xy_peer(d) * self.piece, self.piece)],
                     self.from_xy.at[d - 1], place_of(core, xy_peer(d), z))

        def send_z(self):
            finish(self.first + 1, self.from_xy)
            total = self.held_core[rows(xy * self.piece, self.piece), :]
            for d in range(15):
                total = total + self.from_xy[d]
            self.held_z[...] = total
            self.from_z[z] = total
            for d in far_z:
                push(self.first + 2, self.held_z, self.from_z.at[z], z_peer(d))

        def gather_plane(self):
            finish(self.first + 2, self.from_z.at[0:7])
            total = self.from_z[0]
            for d in range(1, 8):
                total = total + self.from_z[d]
            mine = full.at[rows(self.base + core * self.half + xy * self.piece, self.piece)]
            mine[...] = total
            for d in far_first:
                push(self.first + 3, mine, mine, place_of(core, xy_peer(d), z))

        def gather_core(self):
            finish(self.first + 3, self.from_xy)
            mine = full.at[rows(self.base + core * self.half, self.half)]
            push(self.first + 4, mine, mine, core_peer)

        def end(self):
            finish(self.first + 4, self.from_core)

    third = Stream(0, 0, 32, parts_a, from_core_a, held_core_a, from_xy_a, held_z_a, from_z_a)
    others = Stream(5, 1024, 16, parts_b, from_core_b, held_core_b, from_xy_b, held_z_b, from_z_b)

    take(2)
    pred, delta3 = upward()
    for phase in range(4):
        for half in range(2):
            parts_a[pl.ds(half * 512 + phase, 128, stride=4), :] = (
                g3[phase * 128:phase * 128 + 128, half * 128:half * 128 + 128])
    third.send_core()
    show(2, pred)
    back_third(delta3)
    back_second(0)
    third.send_plane()
    back_second(1)
    for phase in range(4):
        parts_b[pl.ds(phase, 64, stride=4), :] = g2[phase * 64:phase * 64 + 64, :]
    picked = jnp.where(first_mask(), g1[...], 0.0)
    folded = lax.dot_general(
        one_hot(first_spread(), F32), picked, (((1,), (1,)), ((), ())),
        precision=lax.Precision.HIGHEST, preferred_element_type=F32)
    parts_b[256:280, :] = folded[:, :128] + folded[:, 128:256] + folded[:, 256:384] + folded[:, 384:]
    parts_b[280:288, :] = gh[:, :128]
    parts_b[288:296, :] = gh[:, 128:]
    parts_b[296:, :] = jnp.zeros((216, 128), F32)
    others.send_core()
    others.send_plane()
    third.send_z()
    others.send_z()
    third.gather_plane()
    others.gather_plane()
    third.gather_core()
    others.gather_core()
    third.end()
    others.end()
    for which in range(2):
        @pl.when(by_relay[which])
        def passed():
            to_relay(which).wait_send()
            onward(which).wait_send()

    for k in range(8):
        straight = jnp.bool_(True)
        for which in range(2):
            if k in relayed[which]:
                straight = jnp.logical_not(by_relay[which] & (pick(y == 3, *relayed[which]) == k))

        @pl.when(straight)
        def answered():
            reply(jnp.int32(k)).wait_send()


def network(counts, offsets, image, own_target, cut_target, weights):
    vmem = pl.BlockSpec(memory_space=pltpu.VMEM)
    dma = pltpu.SemaphoreType.DMA((8,))
    return pl.pallas_call(
        net_kernel,
        out_shape=(pltpu.VMEM((ROWS, 128), F32), pltpu.VMEM((8, 1024), BF)),
        in_specs=[pl.BlockSpec(memory_space=pltpu.SMEM), vmem] + [pl.BlockSpec(memory_space=pl.ANY)] * 7,
        out_specs=(vmem, vmem),
        scratch_shapes=[
            pltpu.VMEM((6, 128, 256), BF),
            pltpu.VMEM((8, 512), F32),
            pltpu.VMEM((8, 1024), F32),
            pltpu.VMEM((24, 64), BF),
            pltpu.VMEM((256, 128), BF),
            pltpu.VMEM((512, 256), BF),
            pltpu.VMEM((8, 256), BF),
            pltpu.VMEM((8, 8, 128), I32),
            pltpu.VMEM((8, 8, 128), I32),
            pltpu.VMEM((128, 640), BF),
            pltpu.VMEM((6, 640, 256), F32),
            pltpu.VMEM((8, 384, 128), BF),
            pltpu.VMEM((8, 384, 128), BF),
            pltpu.VMEM((2, 384, 128), BF),
            pltpu.VMEM((2, 192, 512), BF),
            pltpu.VMEM((1024, 1024), BF),
            pltpu.VMEM((1024, 1024), BF),
            pltpu.VMEM((512, 192), BF),
            pltpu.VMEM((256, 128), BF),
            pltpu.VMEM((128, 256), BF),
            pltpu.VMEM((512, 256), BF),
            pltpu.VMEM((256, 512), BF),
            pltpu.VMEM((2, 512, 512), BF),
            pltpu.VMEM((2, 512, 512), F32),
            pltpu.VMEM((512, 512), BF),
            pltpu.VMEM((512, 512), F32),
            pltpu.VMEM((2, 512, 512), BF),
            pltpu.VMEM((512, 512), BF),
            pltpu.VMEM((8, 512), F32),
            pltpu.VMEM((8, 512), F32),
            pltpu.VMEM((512, 192), F32),
            pltpu.VMEM((256, 128), F32),
            pltpu.VMEM((512, 256), F32),
            pltpu.VMEM((8, 256), F32),
            pltpu.VMEM((1024, 128), F32),
            pltpu.VMEM((512, 128), F32),
            pltpu.VMEM((512, 128), F32),
            pltpu.VMEM((15, 32, 128), F32),
            pltpu.VMEM((32, 128), F32),
            pltpu.VMEM((8, 32, 128), F32),
            pltpu.VMEM((512, 128), F32),
            pltpu.VMEM((256, 128), F32),
            pltpu.VMEM((256, 128), F32),
            pltpu.VMEM((15, 16, 128), F32),
            pltpu.VMEM((16, 128), F32),
            pltpu.VMEM((8, 16, 128), F32),
            dma, dma, dma, dma, dma,
            pltpu.SemaphoreType.DMA((6,)),
            pltpu.SemaphoreType.DMA((10,)),
            pltpu.SemaphoreType.DMA((10,)),
        ],
        compiler_params=pltpu.CompilerParams(
            collective_id=0, has_side_effects=True, vmem_limit_bytes=VMEM_BYTES
        ),
        name="network",
    )(counts, offsets, image, own_target, cut_target, *weights)


def unpack_kernel(full, shown, o1_ref, o2_ref, o3_ref, oh_ref, cut_pred_ref):
    o3_ref[:, :128] = full[0:512, :]
    o3_ref[:, 128:] = full[512:1024, :]
    o2_ref[...] = full[1024:1280, :]
    first = full[1280:1304, :]
    o1_ref[...] = first[:, :64] + first[:, 64:]
    oh_ref[:, :128] = full[1304:1312, :]
    oh_ref[:, 128:] = full[1312:1320, :]
    cut_pred_ref[...] = shown[...]


def unpack(full, shown):
    vmem = pl.BlockSpec(memory_space=pltpu.VMEM)
    return pl.pallas_call(
        unpack_kernel,
        out_shape=(
            jax.ShapeDtypeStruct((24, 64), F32),
            jax.ShapeDtypeStruct((256, 128), F32),
            jax.ShapeDtypeStruct((512, 256), F32),
            jax.ShapeDtypeStruct((8, 256), F32),
            jax.ShapeDtypeStruct((8, 1024), BF),
        ),
        in_specs=[vmem, vmem],
        out_specs=(vmem,) * 5,
        name="unpack",
    )(pltpu.with_memory_space_constraint(full, pltpu.VMEM), pltpu.with_memory_space_constraint(shown, pltpu.VMEM))


def per_device(sky_tile, request_offset, request_count, tile_target, cut_target, w_first, w_second, w_third, w_head):
    full, cut_pred = network(
        request_count.reshape(-1), request_offset.transpose(0, 1, 3, 4, 2), sky_tile,
        tile_target[0, 0], cut_target[0, 0], (w_first, w_second, w_third, w_head))
    *sums, shown = unpack(full, cut_pred)
    return (*sums, shown[None, None])


def solution(mesh):
    return jax.shard_map(
        per_device,
        mesh=mesh,
        in_specs=(
            P(None, "ty", "tx"),
            P("ty", "tx", None, None, None),
            P("ty", "tx", None),
            P("ty", "tx", None, None),
            P("ty", "tx", None, None),
            P(),
            P(),
            P(),
            P(),
        ),
        out_specs=(P(), P(), P(), P(), P("ty", "tx", None, None)),
        check_vma=False,
    )
```
